128 devices in a mesh: brow: 8 (over x, core), bcol: 16 (over z, y).
Axes of the slice: x: 4, y: 4, z: 4, core: 2. Of those that a mesh axis runs over, the one named last changes fastest.
Arguments:
- forcing: bfloat16 [62, 8192, 2048], P(None, 'brow', 'bcol'), may hold values from -6 to 6
- bottom_level: int32 [8192, 2048], P('brow', 'bcol'), may hold values from 0 to 62
- thickness: float32 [62], replicated, may hold values from 0.25 to 4
- eta_prev: float32 [8, 224, 64, 128], P('brow', 'bcol'), may hold values from -6 to 6
- tropic_map: int32 [128, 16], replicated, may hold values from -1 to 223, as said below
Outputs:
- eta_next: float32 [8, 224, 64, 128], P('brow', 'bcol')
The draws below stay inside these ranges and needn't reach their ends.
Inputs may be any that keep to these rules, and one draw needn't show every extreme that they name: `tropic_map`: each block's owner lies in the band of the block (block rows b * 16 to b * 16 + 15 belong to brow index b); a wet block's value is the owner's bcol index times 14 plus its slot there. Every device owns exactly 14 wet blocks, one in each slot. No clinic device gives more than 2 of its blocks to one owner, and in every band some clinic device gives exactly 2 to some owner.
All inputs are finite; a program needn't handle non-finite values.
Results may differ from the reference program's by a relative error of at most 0.0003.
Values sent between devices are 32-bit elements; how exact they have to be, the bound alone decides.
A program may use at most 128 MiB of HBM per device.

```python
import math
import jax
import jax.numpy as jnp
from jax import lax

BX = 64
BY = 128
BPD = 16
KL = 62
ITERS = 4
CAP = 14
NBR = 128
NBC = 16
NR = 8192
NC = 2048
TSLOTS = 224
BANDS = 8


def draw_tropic_map(key, part):
    pair_count = BPD // 2

    def band_layout(band_key):
        keys = jax.random.split(band_key, 5)
        source_order = jax.random.permutation(keys[0], NBC)
        owner_order = jax.random.permutation(keys[1], NBC)
        local_order = jax.vmap(lambda inner: jax.random.permutation(inner, BPD))(jax.random.split(keys[2], NBC))
        land_pairs = jax.vmap(lambda inner: jax.random.permutation(inner, pair_count))(jax.random.split(keys[3], NBC))
        land_member = jax.random.randint(keys[4], (NBC, 2), 0, 2)
        land_first = 2 * land_pairs[:, 0] + land_member[:, 0]
        land_second = 2 * land_pairs[:, 1] + land_member[:, 1]
        target = (source_order[:, None] + local_order // 2) % NBC
        first = land_first[target]
        second = land_second[target]
        is_land = (local_order == first) | (local_order == second)
        slot = local_order - (first < local_order).astype(jnp.int32) - (second < local_order).astype(jnp.int32)
        position = owner_order[target] * CAP + slot
        return jnp.where(is_land, -1, position).T
    layout = jax.vmap(band_layout)(jax.random.split(key, BANDS))
    return layout.reshape(NBR, NBC).astype(jnp.int32)


def set_ends(result, key, low, high):
    shape = result.shape
    index_at = [jax.random.randint(jax.random.fold_in(key, axis), (), 0, shape[axis]) for axis in range(len(shape))]
    result = result.at[tuple(index_at)].set(low)
    longest = shape.index(max(shape))
    index_at[longest] = (index_at[longest] + 1) % shape[longest]
    return result.at[tuple(index_at)].set(high)


def levels(stream_key, extent, cuts, least, top_value):
    loudness, own = 1.0, jax.random.fold_in(stream_key, 6)
    for dim, blocks in cuts:
        steps = jnp.exp(jax.random.uniform(jax.random.fold_in(own, dim), (blocks,), jnp.float32, least / len(cuts), top_value / len(cuts)))
        loudness = loudness * jnp.repeat(steps, extent[dim] // blocks).reshape([-1 if axis == dim else 1 for axis in range(len(extent))])
    return loudness


def noise(key, shape, spread, reach, cuts=(), kind=jnp.bfloat16):
    level = levels(key, shape, cuts, -0.22, 0.18) if cuts else 1.0
    array = jax.random.normal(key, shape, jnp.float32) * spread * level
    return jnp.minimum(jnp.maximum(array, -reach), reach).astype(kind)


def setup_inputs(seed: int = 0) -> dict:
    key_list = jax.random.split(jax.random.key(seed), 6)
    return {
        "forcing": noise(key_list[0], (KL, NR, NC), 1.0, 6.0, ((1, 8), (2, 16))),
        "bottom_level": set_ends(jax.random.randint(key_list[1], (NR, NC), 0, KL + 1), jax.random.fold_in(key_list[1], 1), 0, KL).astype(jnp.int32),
        "thickness": jnp.clip(jnp.exp(jax.random.uniform(key_list[2], (KL,), jnp.float32, math.log(0.25), math.log(4.0))), 0.25, 4.0),
        "eta_prev": noise(key_list[3], (BANDS, TSLOTS, BX, BY), 1.0, 6.0, ((0, 8), (1, 16)), jnp.float32),
        "tropic_map": draw_tropic_map(jax.random.fold_in(key_list[5], 71), 0),
    }


surface_term = 0.25
neighbour_offsets = ((-1, 0, 1.0), (1, 0, 1.0), (0, -1, 1.0), (0, 1, 1.0), (-1, -1, 0.5), (-1, 1, 0.5), (1, -1, 0.5), (1, 1, 0.5))

def pad_global(field):
    wrapped = jnp.concatenate([field[:, -1:], field, field[:, :1]], axis=1)
    return jnp.pad(wrapped, ((1, 1), (0, 0)))

def shifted(padded, row_shift, col_shift, height, width):
    return padded[..., 1 + row_shift:1 + row_shift + height, 1 + col_shift:1 + col_shift + width]

def reference(forcing, bottom_level, thickness, eta_prev, tropic_map):

    def add_level(carry, inputs):
        depth_sum, source_sum = carry
        layer, layer_thickness, level_id = inputs
        wet_level = level_id < bottom_level
        depth_sum = depth_sum + jnp.where(wet_level, layer_thickness, 0.0)
        source_sum = source_sum + jnp.where(wet_level, layer_thickness * layer.astype(jnp.float32), 0.0)
        return ((depth_sum, source_sum), None)
    zero_field = jnp.zeros(bottom_level.shape, jnp.float32)
    (depth_sum, source_sum), unused_out = lax.scan(add_level, (zero_field, zero_field), (forcing, thickness, jnp.arange(KL, dtype=jnp.int32)))
    block_wet = tropic_map >= 0
    cell_mask = jnp.repeat(jnp.repeat(block_wet.astype(jnp.float32), BX, axis=0), BY, axis=1)
    depth = depth_sum / KL * cell_mask
    source = source_sum / math.sqrt(KL) * cell_mask
    band_of_row = jnp.arange(NBR, dtype=jnp.int32) // BPD
    safe_position = jnp.where(block_wet, tropic_map, 0)
    start_blocks = eta_prev[band_of_row[:, None], safe_position] * block_wet.astype(jnp.float32)[:, :, None, None]
    eta_start = start_blocks.transpose(0, 2, 1, 3).reshape(NR, NC)
    padded_depth = pad_global(depth)
    terms = []
    diagonal = surface_term + depth
    for row_shift, col_shift, weight in neighbour_offsets:
        term = weight * (depth + shifted(padded_depth, row_shift, col_shift, NR, NC)) * 0.5
        terms.append(term)
        diagonal = diagonal + term
    rhs = (surface_term + depth) * eta_start + source
    eta = eta_start
    for iteration in range(ITERS):
        padded_eta = pad_global(eta)
        total = rhs
        for (row_shift, col_shift, weight), term in zip(neighbour_offsets, terms):
            total = total + term * shifted(padded_eta, row_shift, col_shift, NR, NC)
        eta = cell_mask * (total / diagonal)
    blocks = eta.reshape(NBR, BX, NBC, BY).transpose(0, 2, 1, 3)
    target = jnp.where(block_wet, tropic_map, TSLOTS)
    band_ids = jnp.broadcast_to(band_of_row[:, None], (NBR, NBC))
    eta_next = jnp.zeros((BANDS, TSLOTS, BX, BY), jnp.float32).at[band_ids, target].set(blocks, mode='drop')
    return eta_next
```

```python
import functools
import math

import jax
import jax.numpy as jnp
from jax import lax
from jax.experimental import pallas as pl
from jax.experimental.pallas import tpu as pltpu
from jax.sharding import PartitionSpec as P

MESH = pl.DeviceIdType.MESH
ITERS = 4
PAIR = 2
HALO = 4
EDGE = 8
PAD = 16
CHUNK = 40
SURFACE = 0.25


def kernel(
    sizes,
    tropic_map, thickness, forcing, bottom_level, eta_prev,
    eta_next,
    forcing_v, bottom_v, prev_v,
    send_in, recv_in, send_out, recv_out,
    half, source, rhs, inverse, eta, eta_end, t_eta, t_half, rest,
    pack_src, pack_eta, col_src, col_eta,
    edge_src, edge_eta, row_src, row_eta,
    t_in, t_clinic, t_out, t_owner, owner_of,
    load_sem, prev_sem, bottom_sem,
    in_send, in_recv, out_send, out_recv,
    halo_send, halo_recv,
):
    columns, bands, block_rows, rows, levels, slots, width = sizes
    blocks = rows // block_rows
    band = lax.axis_index("brow")
    me = lax.axis_index("bcol")
    first_row = band * blocks
    base = me * slots

    pltpu.make_async_copy(eta_prev.at[0], prev_v, prev_sem).start()
    pltpu.make_async_copy(bottom_level, bottom_v, bottom_sem).start()

    def load(block):
        span = pl.ds(pl.multiple_of(block * block_rows, block_rows), block_rows)
        return pltpu.make_async_copy(
            forcing.at[:, span, :], forcing_v.at[:, span, :], load_sem.at[block]
        )

    @pl.loop(0, blocks)
    def _(block):
        load(block).start()

    def column_at(shift):
        return lax.rem(me + shift + columns, columns)

    def band_at(shift):
        return lax.rem(band + shift + bands, bands)

    barrier = pltpu.get_barrier_semaphore()

    @pl.loop(1, columns)
    def _(shift):
        pl.semaphore_signal(barrier, inc=1, device_id=(band, column_at(shift)), device_id_type=MESH)

    beside = [(up, across) for up in (-1, 1) for across in (-1, 0, 1)]
    for up, across in beside:
        pl.semaphore_signal(
            barrier, inc=1, device_id=(band_at(up), column_at(across)), device_id_type=MESH
        )

    @pl.loop(0, columns)
    def _(column):
        first, second = jnp.int32(-1), jnp.int32(-1)
        for block in reversed(range(blocks)):
            slot = tropic_map[first_row + block, column] - base
            mine = (slot >= 0) & (slot < slots)
            second = jnp.where(mine, first, second)
            first = jnp.where(mine, slot, first)
        t_in[PAIR * column] = first
        t_in[PAIR * column + 1] = second

    pltpu.make_async_copy(eta_prev.at[0], prev_v, prev_sem).wait()

    def gather_in(peer):
        for rank in range(PAIR):
            index = jnp.maximum(t_in[PAIR * peer + rank], 0)
            yield rank, prev_v[index]

    @pl.loop(1, columns)
    def _(shift):
        for rank, value in gather_in(column_at(shift)):
            send_in[PAIR * shift + rank] = value

    for rank, value in gather_in(me):
        recv_in[PAIR * me + rank] = value

    pl.semaphore_wait(barrier, columns - 1 + len(beside))

    def exchange(shift, sent, received, send_sem, recv_sem):
        peer = column_at(shift)
        return pltpu.make_async_remote_copy(
            src_ref=sent.at[pl.ds(PAIR * shift, PAIR)],
            dst_ref=received.at[pl.ds(PAIR * me, PAIR)],
            send_sem=send_sem.at[shift],
            recv_sem=recv_sem.at[shift],
            device_id=(band, peer),
            device_id_type=MESH,
        )

    @pl.loop(1, columns)
    def _(shift):
        exchange(shift, send_in, recv_in, in_send, in_recv).start()

    lane = lax.broadcasted_iota(jnp.int32, (block_rows, width), 1)
    group = lane // HALO
    pltpu.make_async_copy(bottom_level, bottom_v, bottom_sem).wait()
    pack_src[...] = jnp.zeros_like(pack_src)

    @pl.loop(0, blocks)
    def _(block):
        load(block).wait()
        start = pl.multiple_of(block * block_rows, block_rows)
        span = pl.ds(start, block_rows)
        bottom = bottom_v[span, :]

        def level(number, carry):
            depth_sum, source_sum = carry
            for step in range(2):
                k = number * 2 + step
                layer = forcing_v[k, span, :].astype(jnp.float32)
                thick = jnp.where(bottom > k, thickness[k], 0.0)
                depth_sum = depth_sum + thick
                source_sum = source_sum + thick * layer
            return depth_sum, source_sum

        zero = jnp.zeros((block_rows, width), jnp.float32)
        depth_sum, source_sum = lax.fori_loop(0, levels // 2, level, (zero, zero))
        wet = jnp.where(tropic_map[first_row + block, me] >= 0, 1.0, 0.0)
        half_depth = depth_sum * (wet * (0.5 / levels))
        src = source_sum * (wet * (1.0 / math.sqrt(levels)))
        here = pl.ds(pl.multiple_of(EDGE + start, EDGE), block_rows)
        half[0, here, :] = half_depth
        source[0, here, :] = src
        for side, turn in ((0, 0), (1, HALO)):
            moved_half = pltpu.roll(half_depth, HALO * block + turn, 1)
            moved_src = pltpu.roll(src, HALO * block + turn + width // 2, 1)
            packed = pack_src[side]
            packed = jnp.where(group == block, moved_half, packed)
            packed = jnp.where(group == block + width // 2 // HALO, moved_src, packed)
            pack_src[side] = packed

    edge_src[0, 0] = half[0, pl.ds(EDGE, EDGE), :]
    edge_src[0, 1] = source[0, pl.ds(EDGE, EDGE), :]
    edge_src[1, 0] = half[0, pl.ds(rows, EDGE), :]
    edge_src[1, 1] = source[0, pl.ds(rows, EDGE), :]

    def halo_copies(stage, pack, col, edge, row):
        copies = []
        for side, across in ((0, -1), (1, 1)):
            number = 8 * stage + side
            copies.append(
                pltpu.make_async_remote_copy(
                    src_ref=pack.at[side],
                    dst_ref=col.at[side],
                    send_sem=halo_send.at[number],
                    recv_sem=halo_recv.at[number],
                    device_id=(band, column_at(across)),
                    device_id_type=MESH,
                )
            )
        for place, (up, across) in enumerate(beside):
            number = 8 * stage + 2 + place
            copies.append(
                pltpu.make_async_remote_copy(
                    src_ref=edge.at[0 if up < 0 else 1],
                    dst_ref=row.at[place],
                    send_sem=halo_send.at[number],
                    recv_sem=halo_recv.at[number],
                    device_id=(band_at(up), column_at(across)),
                    device_id_type=MESH,
                )
            )
        return copies

    first_halos = halo_copies(0, pack_src, col_src, edge_src, row_src)
    for copy in first_halos:
        copy.start()

    for block in range(blocks):
        value = tropic_map[first_row + block, me]
        owner_of[block] = jnp.where(value >= 0, value // slots, -1)
    for block in range(blocks):
        owner = owner_of[block]
        rank = jnp.int32(0)
        for before in range(block):
            rank = jnp.where(owner_of[before] == owner, 1, rank)
        t_clinic[block] = jnp.where(owner >= 0, owner * PAIR + rank, 0)

    @pl.loop(0, columns)
    def _(owner):
        first, second = jnp.int32(0), jnp.int32(0)
        for block in reversed(range(blocks)):
            mine = owner_of[block] == owner
            second = jnp.where(mine, first, second)
            first = jnp.where(mine, block, first)
        t_out[PAIR * owner] = first
        t_out[PAIR * owner + 1] = second

    @pl.loop(0, slots)
    def _(slot):
        place = jnp.int32(0)
        for entry in range(PAIR * columns):
            place = jnp.where(t_in[entry] == slot, entry, place)
        t_owner[slot] = place

    for copy in first_halos:
        copy.wait()

    has_above = jnp.where(band > 0, 1.0, 0.0)
    has_below = jnp.where(band < bands - 1, 1.0, 0.0)
    edge_lane = lax.broadcasted_iota(jnp.int32, (EDGE, width), 1) < width // 2
    edges = (
        (0, 3, has_above),
        (EDGE + rows, 0, has_below),
    )

    def edge_rows(field, arrived):
        for at, place, inside in edges:
            there = pl.ds(at, EDGE)
            right, middle, left = (arrived(place + k) for k in range(3))
            field[0, there, :] = middle * inside
            field[1, there, :] = jnp.where(edge_lane, right, left) * inside

    edge_rows(half, lambda place: row_src[place, 0])
    edge_rows(source, lambda place: row_src[place, 1])

    right_half = lane < width // 2

    @pl.loop(0, blocks)
    def _(block):
        here = pl.ds(pl.multiple_of(EDGE + block * block_rows, EDGE), block_rows)
        for field, turn in ((half, 0), (source, width // 2)):
            from_right = pltpu.roll(col_src[0], 2 * width - HALO * block - turn, 1)
            from_left = pltpu.roll(col_src[1], 2 * width - HALO * (block + 1) - turn, 1)
            field[1, here, :] = jnp.where(right_half, from_right, from_left)

    total_rows = rows + 2 * EDGE
    chunk_lane = lax.broadcasted_iota(jnp.int32, (CHUNK, width), 1)

    def beside_sum(main, side):
        at_end, at_start = chunk_lane == width - 1, chunk_lane == 0
        main_sum = pltpu.roll(jnp.where(at_end, side, main), 1, 1) + pltpu.roll(
            jnp.where(at_start, side, main), width - 1, 1
        )
        side_sum = pltpu.roll(jnp.where(at_end, main, side), 1, 1) + pltpu.roll(
            jnp.where(at_start, main, side), width - 1, 1
        )
        return main_sum, side_sum

    @pl.loop(0, total_rows // CHUNK)
    def _(chunk):
        start = pl.multiple_of(chunk * CHUNK, EDGE)
        here, there = pl.ds(start, CHUNK), pl.ds(pl.multiple_of(start + EDGE, EDGE), CHUNK)
        sums = beside_sum(half[0, here, :], half[1, here, :])
        for part in range(2):
            value = half[part, here, :]
            t_half[part, there, :] = value + 0.5 * sums[part]
            rest[part, here, :] = (SURFACE + 8.0 * value) + sums[part]

    @pl.loop(0, total_rows // CHUNK)
    def _(chunk):
        start = pl.multiple_of(chunk * CHUNK, EDGE)
        here = pl.ds(start, CHUNK)
        above, below = pl.ds(start + EDGE - 1, CHUNK), pl.ds(start + EDGE + 1, CHUNK)
        for part in range(2):
            total = rest[part, here, :] + (t_half[part, above, :] + t_half[part, below, :])
            inverse[part, here, :] = 1.0 / total

    right_column, left_column = column_at(1), column_at(-1)

    def wet_of(row, column):
        return jnp.where(tropic_map[row, column] >= 0, 1.0, 0.0)

    @pl.loop(0, blocks)
    def _(block):
        here = pl.ds(pl.multiple_of(EDGE + block * block_rows, EDGE), block_rows)
        row = first_row + block
        inverse[0, here, :] = inverse[0, here, :] * wet_of(row, me)
        inverse[1, here, :] = inverse[1, here, :] * jnp.where(
            right_half, wet_of(row, right_column), wet_of(row, left_column)
        )

    above_row = jnp.maximum(first_row - 1, 0)
    below_row = jnp.minimum(first_row + blocks, bands * blocks - 1)
    for (at, _, inside), row in zip(edges, (above_row, below_row)):
        there = pl.ds(at, EDGE)
        inverse[0, there, :] = inverse[0, there, :] * (wet_of(row, me) * inside)
        inverse[1, there, :] = inverse[1, there, :] * (
            jnp.where(edge_lane, wet_of(row, right_column), wet_of(row, left_column)) * inside
        )

    @pl.loop(1, columns)
    def _(shift):
        exchange(shift, send_in, recv_in, in_send, in_recv).wait()

    pack_eta[...] = jnp.zeros_like(pack_eta)

    @pl.loop(0, blocks)
    def _(block):
        here = pl.ds(pl.multiple_of(EDGE + block * block_rows, EDGE), block_rows)
        value = recv_in[t_clinic[block]] * wet_of(first_row + block, me)
        eta[0, here, :] = value
        first = pltpu.roll(value, HALO * block, 1)
        last = pltpu.roll(value, HALO * block + HALO + width // 2, 1)
        packed = pack_eta[0]
        packed = jnp.where(group == block, first, packed)
        packed = jnp.where(group == block + width // 2 // HALO, last, packed)
        pack_eta[0] = packed

    pack_eta[1] = pack_eta[0]
    edge_eta[0] = eta[0, pl.ds(EDGE, EDGE), :]
    edge_eta[1] = eta[0, pl.ds(rows, EDGE), :]
    second_halos = halo_copies(1, pack_eta, col_eta, edge_eta, row_eta)
    for copy in second_halos:
        copy.start()
    for copy in second_halos:
        copy.wait()

    edge_rows(eta, lambda place: row_eta[place])

    @pl.loop(0, blocks)
    def _(block):
        here = pl.ds(pl.multiple_of(EDGE + block * block_rows, EDGE), block_rows)
        from_right = pltpu.roll(col_eta[0], 2 * width - HALO * block, 1)
        from_left = pltpu.roll(col_eta[1], 2 * width - HALO * (block + 1) - width // 2, 1)
        eta[1, here, :] = jnp.where(right_half, from_right, from_left)

    @pl.loop(0, total_rows // CHUNK)
    def _(chunk):
        here = pl.ds(pl.multiple_of(chunk * CHUNK, EDGE), CHUNK)
        for part in range(2):
            rhs[part, here, :] = (SURFACE + 2.0 * half[part, here, :]) * eta[
                part, here, :
            ] + source[part, here, :]

    def spread():
        @pl.loop(0, total_rows // CHUNK)
        def _(chunk):
            start = pl.multiple_of(chunk * CHUNK, EDGE)
            here, there = pl.ds(start, CHUNK), pl.ds(pl.multiple_of(start + EDGE, EDGE), CHUNK)
            values = [eta[part, here, :] for part in range(2)]
            halves = [half[part, here, :] for part in range(2)]
            scaled = [value * weight for value, weight in zip(values, halves)]
            sums = beside_sum(*values)
            scaled_sums = beside_sum(*scaled)
            for part in range(2):
                t_eta[part, there, :] = values[part] + 0.5 * sums[part]
                t_half[part, there, :] = scaled[part] + 0.5 * scaled_sums[part]
                rest[part, here, :] = (
                    rhs[part, here, :] + halves[part] * sums[part] + scaled_sums[part]
                )

    def settle(part, start, count):
        here = pl.ds(start, count)
        above, below = pl.ds(start + EDGE - 1, count), pl.ds(start + EDGE + 1, count)
        total = rest[part, here, :] + (t_half[part, above, :] + t_half[part, below, :])
        total = total + half[part, here, :] * (t_eta[part, above, :] + t_eta[part, below, :])
        return total * inverse[part, here, :]

    @pl.loop(0, ITERS - 1)
    def _(iteration):
        spread()

        @pl.loop(0, total_rows // CHUNK)
        def _(chunk):
            start = pl.multiple_of(chunk * CHUNK, EDGE)
            for part in range(2):
                eta[part, pl.ds(start, CHUNK), :] = settle(part, start, CHUNK)

    spread()

    @pl.loop(0, blocks)
    def _(block):
        start = pl.multiple_of(EDGE + block * block_rows, EDGE)
        eta_end[block] = settle(0, start, block_rows)

    @pl.loop(1, columns)
    def _(shift):
        peer = column_at(shift)
        for rank in range(PAIR):
            send_out[PAIR * shift + rank] = eta_end[t_out[PAIR * peer + rank]]
        exchange(shift, send_out, recv_out, out_send, out_recv).start()

    for rank in range(PAIR):
        recv_out[PAIR * me + rank] = eta_end[t_out[PAIR * me + rank]]

    @pl.loop(1, columns)
    def _(shift):
        exchange(shift, send_out, recv_out, out_send, out_recv).wait()

    @pl.loop(0, slots)
    def _(slot):
        eta_next[0, slot] = recv_out[t_owner[slot]]


def solution(mesh):
    columns, bands = mesh.shape["bcol"], mesh.shape["brow"]

    def body(forcing, bottom_level, thickness, eta_prev, tropic_map):
        levels, rows, width = forcing.shape
        slots, block_rows = eta_prev.shape[1], eta_prev.shape[2]
        blocks = rows // block_rows
        sizes = (columns, bands, block_rows, rows, levels, slots, width)
        f32 = jnp.float32
        padded, more = rows + 2 * EDGE, rows + 2 * PAD
        dma = pltpu.SemaphoreType.DMA
        scratch = [
            pltpu.VMEM(forcing.shape, forcing.dtype),
            pltpu.VMEM((rows, width), jnp.int32),
            pltpu.VMEM((slots, block_rows, width), f32),
        ]
        scratch += [pltpu.VMEM((PAIR * columns, block_rows, width), f32)] * 4
        scratch += [pltpu.VMEM((2, padded, width), f32)] * 5
        scratch += [pltpu.VMEM((blocks, block_rows, width), f32)]
        scratch += [pltpu.VMEM((2, more, width), f32)] * 2
        scratch += [pltpu.VMEM((2, padded, width), f32)]
        scratch += [pltpu.VMEM((2, block_rows, width), f32)] * 4
        scratch += [pltpu.VMEM((2, 2, EDGE, width), f32), pltpu.VMEM((2, EDGE, width), f32)]
        scratch += [pltpu.VMEM((6, 2, EDGE, width), f32), pltpu.VMEM((6, EDGE, width), f32)]
        scratch += [
            pltpu.SMEM((count,), jnp.int32)
            for count in (PAIR * columns, blocks, PAIR * columns, slots, blocks)
        ]
        scratch += [dma((blocks,)), dma, dma]
        scratch += [dma((columns,))] * 4
        scratch += [dma((16,))] * 2
        hbm = pl.BlockSpec(memory_space=pl.ANY)
        smem = pl.BlockSpec(memory_space=pltpu.SMEM)
        return pl.pallas_call(
            functools.partial(kernel, sizes),
            out_shape=jax.ShapeDtypeStruct(eta_prev.shape, f32),
            in_specs=[smem, smem, hbm, hbm, hbm],
            out_specs=pl.BlockSpec(memory_space=pltpu.VMEM),
            scratch_shapes=scratch,
            compiler_params=pltpu.CompilerParams(
                collective_id=0, has_side_effects=True, vmem_limit_bytes=56 * 1024 * 1024
            ),
            cost_estimate=pl.CostEstimate(
                flops=60_000_000, bytes_accessed=18_000_000, transcendentals=0
            ),
        )(tropic_map, thickness, forcing, bottom_level, eta_prev)

    in_specs = (P(None, "brow", "bcol"), P("brow", "bcol"), P(), P("brow", "bcol", None, None), P())
    out_specs = P("brow", "bcol", None, None)
    return jax.shard_map(body, mesh=mesh, in_specs=in_specs, out_specs=out_specs, check_vma=False)
```

```python
import functools
import math

import jax
import jax.numpy as jnp
from jax import lax
from jax.experimental import pallas as pl
from jax.experimental.pallas import tpu as pltpu
from jax.sharding import PartitionSpec as P

MESH = pl.DeviceIdType.MESH
ITERS = 4
PAIR = 2
HALO = 4
TILE = 8
FINE = 9
SURFACE = 0.25


def kernel(
    sizes,
    tropic_map, thickness, forcing, bottom_level, eta_prev,
    eta_next,
    forcing_v, bottom_v, prev_v,
    send_in, recv_in, send_out, recv_out, eta_end,
    nat_half, nat_source, nat_eta, corner,
    raw, half, source, rhs, inverse, eta, rest,
    g_eta, g_half,
    strip_first, strip_eta, col_first, col_eta,
    edge_first, row_first, row_eta,
    map_v, thick,
    t_in, t_clinic, t_out, t_owner, owner_of,
    load_sem, prev_sem, bottom_sem, map_sem, thick_sem,
    in_send, in_recv, out_send, out_recv,
    halo_send, halo_recv,
):
    columns, bands, block_rows, rows, levels, slots, width = sizes
    blocks = rows // block_rows
    band = lax.axis_index("brow")
    me = lax.axis_index("bcol")
    base = me * slots
    first_row = band * blocks

    def column_at(shift):
        return lax.rem(me + shift + columns, columns)

    def band_at(shift):
        return lax.rem(band + shift + bands, bands)

    barrier = pltpu.get_barrier_semaphore()

    @pl.loop(1, columns)
    def _(shift):
        pl.semaphore_signal(barrier, inc=1, device_id=(band, column_at(shift)), device_id_type=MESH)

    beside = [(up, across) for up in (-1, 1) for across in (-1, 0, 1)]
    for up, across in beside:
        pl.semaphore_signal(
            barrier, inc=1, device_id=(band_at(up), column_at(across)), device_id_type=MESH
        )

    map_copy = pltpu.make_async_copy(tropic_map, map_v, map_sem)
    prev_copy = pltpu.make_async_copy(eta_prev.at[0], prev_v, prev_sem)
    thick_copy = pltpu.make_async_copy(thickness, thick, thick_sem)
    bottom_copy = pltpu.make_async_copy(bottom_level, bottom_v, bottom_sem)
    for copy in (map_copy, prev_copy, thick_copy, bottom_copy):
        copy.start()

    def load(block):
        span = pl.ds(pl.multiple_of(block * block_rows, block_rows), block_rows)
        return pltpu.make_async_copy(
            forcing.at[:, span, :], forcing_v.at[:, span, :], load_sem.at[block]
        )

    @pl.loop(0, blocks)
    def _(block):
        load(block).start()

    map_copy.wait()

    @pl.loop(0, columns)
    def _(column):
        first, second = jnp.int32(-1), jnp.int32(-1)
        for block in reversed(range(blocks)):
            slot = map_v[column, first_row + block] - base
            mine = (slot >= 0) & (slot < slots)
            second = jnp.where(mine, first, second)
            first = jnp.where(mine, slot, first)
        t_in[PAIR * column] = first
        t_in[PAIR * column + 1] = second

    prev_copy.wait()

    def gather_in(peer):
        for rank in range(PAIR):
            index = jnp.maximum(t_in[PAIR * peer + rank], 0)
            yield rank, prev_v[index]

    @pl.loop(1, columns)
    def _(shift):
        for rank, value in gather_in(column_at(shift)):
            send_in[PAIR * shift + rank] = value

    for rank, value in gather_in(me):
        recv_in[PAIR * me + rank] = value

    pl.semaphore_wait(barrier, columns - 1 + len(beside))

    def exchange(shift, sent, received, send_sem, recv_sem):
        peer = column_at(shift)
        return pltpu.make_async_remote_copy(
            src_ref=sent.at[pl.ds(PAIR * shift, PAIR)],
            dst_ref=received.at[pl.ds(PAIR * me, PAIR)],
            send_sem=send_sem.at[shift],
            recv_sem=recv_sem.at[shift],
            device_id=(band, peer),
            device_id_type=MESH,
        )

    @pl.loop(1, columns)
    def _(shift):
        exchange(shift, send_in, recv_in, in_send, in_recv).start()

    thick_copy.wait()
    bottom_copy.wait()

    @pl.loop(0, blocks)
    def _(block):
        load(block).wait()
        start = pl.multiple_of(block * block_rows, block_rows)
        span = pl.ds(start, block_rows)
        bottom = bottom_v[span, :]

        def level(number, carry):
            depth_sum, source_sum = carry
            for step in range(2):
                k = number * 2 + step
                layer = forcing_v[k, span, :].astype(jnp.float32)
                weight = jnp.where(bottom > k, thick[k], 0.0)
                depth_sum = depth_sum + weight
                source_sum = source_sum + weight * layer
            return depth_sum, source_sum

        zero = jnp.zeros((block_rows, width), jnp.float32)
        depth_sum, source_sum = lax.fori_loop(0, levels // 2, level, (zero, zero))
        wet = jnp.where(map_v[me, first_row + block] >= 0, 1.0, 0.0)
        here = pl.ds(pl.multiple_of(TILE + start, TILE), block_rows)
        nat_half[here, :] = depth_sum * (wet * (0.5 / levels)) + (wet - 1.0)
        nat_source[here, :] = source_sum * (wet * (1.0 / math.sqrt(levels)))

    def remote(number, src, dst, device):
        return pltpu.make_async_remote_copy(
            src_ref=src,
            dst_ref=dst,
            send_sem=halo_send.at[number],
            recv_sem=halo_recv.at[number],
            device_id=device,
            device_id_type=MESH,
        )

    def row_copies(stage, top, bottom, row):
        return [
            remote(
                8 * stage + 2 + place,
                top if up < 0 else bottom,
                row.at[place],
                (band_at(up), column_at(across)),
            )
            for place, (up, across) in enumerate(beside)
        ]

    def col_copies(stage, strip, col):
        return [
            remote(8 * stage + side, strip, col.at[side], (band, column_at(across)))
            for side, across in ((0, -1), (1, 1))
        ]

    has_above = jnp.where(band > 0, 1.0, 0.0)
    has_below = jnp.where(band < bands - 1, 1.0, 0.0)
    tile_lane = lax.broadcasted_iota(jnp.int32, (TILE, width), 1)
    low_lane = tile_lane < width // 2
    low_row = lax.broadcasted_iota(jnp.int32, (TILE, width), 0) < HALO
    low_rows = lax.broadcasted_iota(jnp.int32, (FINE, TILE, width), 1) < HALO
    above_at, below_at = 0, TILE + rows
    near = [(n, n) for n in range(TILE - HALO, TILE)]
    near += [(below_at + m, TILE + m) for m in range(HALO)]
    fine_near = sorted({n % FINE for n, _ in near})
    last = width - TILE
    side_rows = pl.ds(width, TILE)

    def turn(nat, field, fine):
        for f in fine:
            field[f, pl.ds(0, width), :] = nat[pl.ds(f, width, stride=FINE), :].T

    def strip_of(field):
        return jnp.where(low_rows, field[:, pl.ds(0, TILE), :], field[:, pl.ds(last, TILE), :])

    def fill(nat, field, arrived_row, arrived_col, outside):
        for at, place, inside in ((above_at, 3, has_above), (below_at, 0, has_below)):
            right, middle, left = (arrived_row(place + k) for k in range(3))
            absent = (1.0 - inside) * outside
            nat[pl.ds(at, TILE), :] = middle * inside + absent
            side = jnp.where(low_lane, right, left) * inside + absent
            corner[pl.ds(TILE if at else 0, TILE), :] = side
        turn(nat, field, fine_near)
        turned = corner[...].T
        sides = jnp.where(low_row, turned[0:TILE, :], turned[last:width, :])
        field[:, side_rows, :] = jnp.where(low_rows, arrived_col(0), arrived_col(1))
        for n, lane in near:
            f, to = n % FINE, n // FINE
            moved = pltpu.roll(sides, (to - lane) % width, 1)
            field[f, side_rows, :] = jnp.where(tile_lane == to, moved, field[f, side_rows, :])

    corner[...] = jnp.zeros_like(corner)
    for number, nat in enumerate((nat_half, nat_source)):
        edge_first[0, number] = nat[pl.ds(TILE, TILE), :]
        edge_first[1, number] = nat[pl.ds(rows, TILE), :]
    first_rows = row_copies(0, edge_first.at[0], edge_first.at[1], row_first)
    for copy in first_rows:
        copy.start()
    turn(nat_half, raw, range(FINE))
    turn(nat_source, source, range(FINE))
    strip_first[0] = strip_of(raw)
    strip_first[1] = strip_of(source)
    first_cols = col_copies(0, strip_first, col_first)
    for copy in first_cols:
        copy.start()

    for block in range(blocks):
        value = map_v[me, first_row + block]
        owner_of[block] = jnp.where(value >= 0, value // slots, -1)
    for block in range(blocks):
        owner = owner_of[block]
        rank = jnp.int32(0)
        for before in range(block):
            rank = jnp.where(owner_of[before] == owner, 1, rank)
        t_clinic[block] = jnp.where(owner >= 0, owner * PAIR + rank, 0)

    @pl.loop(0, columns)
    def _(owner):
        first, second = jnp.int32(0), jnp.int32(0)
        for block in reversed(range(blocks)):
            mine = owner_of[block] == owner
            second = jnp.where(mine, first, second)
            first = jnp.where(mine, block, first)
        t_out[PAIR * owner] = first
        t_out[PAIR * owner + 1] = second

    @pl.loop(0, slots)
    def _(slot):
        place = jnp.int32(0)
        for entry in range(PAIR * columns):
            place = jnp.where(t_in[entry] == slot, entry, place)
        t_owner[slot] = place

    for copy in first_rows + first_cols:
        copy.wait()
    fill(nat_half, raw, lambda p: row_first[p, 0], lambda s: col_first[s, 0], -1.0)
    fill(nat_source, source, lambda p: row_first[p, 1], lambda s: col_first[s, 1], 0.0)

    tiles = width // TILE + 1

    def tile_at(tile):
        return pl.ds(TILE * tile, TILE)

    def row_sum(value):
        before = jnp.concatenate([pltpu.roll(value[FINE - 1 :], 1, 2), value[: FINE - 1]], axis=0)
        after = jnp.concatenate([value[1:], pltpu.roll(value[:1], width - 1, 2)], axis=0)
        return before + after

    def put(field, tile, value):
        field[:, tile_at(tile + 1), :] = value
        if tile == tiles - 1:
            field[:, tile_at(0), :] = value
        if tile == 0:
            field[:, tile_at(tiles + 1), :] = value

    def col_sum(field, tile):
        start = TILE * (tile + 1)
        return field[:, pl.ds(start - 1, TILE), :] + field[:, pl.ds(start + 1, TILE), :]

    for tile in range(tiles):
        value = jnp.maximum(raw[:, tile_at(tile), :], 0.0)
        half[:, tile_at(tile), :] = value
        around = row_sum(value)
        put(g_half, tile, value + 0.5 * around)
        rest[:, tile_at(tile), :] = (SURFACE + 8.0 * value) + around
    for tile in range(tiles):
        diagonal = rest[:, tile_at(tile), :] + col_sum(g_half, tile)
        wet = raw[:, tile_at(tile), :] >= 0.0
        inverse[:, tile_at(tile), :] = jnp.where(wet, 1.0 / diagonal, 0.0)

    @pl.loop(1, columns)
    def _(shift):
        exchange(shift, send_in, recv_in, in_send, in_recv).wait()

    for block in range(blocks):
        wet = jnp.where(map_v[me, first_row + block] >= 0, 1.0, 0.0)
        nat_eta[pl.ds(TILE + block * block_rows, block_rows), :] = recv_in[t_clinic[block]] * wet

    second_rows = row_copies(
        1, nat_eta.at[pl.ds(TILE, TILE)], nat_eta.at[pl.ds(rows, TILE)], row_eta
    )
    for copy in second_rows:
        copy.start()
    turn(nat_eta, eta, range(FINE))
    strip_eta[...] = strip_of(eta)
    second_cols = col_copies(1, strip_eta, col_eta)
    for copy in second_cols:
        copy.start()
    for copy in second_rows + second_cols:
        copy.wait()
    fill(nat_eta, eta, lambda p: row_eta[p], lambda s: col_eta[s], 0.0)
    for tile in range(tiles):
        here = tile_at(tile)
        rhs[:, here, :] = (SURFACE + 2.0 * half[:, here, :]) * eta[:, here, :] + source[:, here, :]

    @pl.loop(0, ITERS)
    def _(iteration):
        for tile in range(tiles):
            here = tile_at(tile)
            value, weight = eta[:, here, :], half[:, here, :]
            scaled = value * weight
            around, scaled_around = row_sum(value), row_sum(scaled)
            put(g_eta, tile, value + 0.5 * around)
            put(g_half, tile, scaled + 0.5 * scaled_around)
            rest[:, here, :] = rhs[:, here, :] + weight * around + scaled_around
        for tile in range(tiles):
            here = tile_at(tile)
            total = rest[:, here, :] + col_sum(g_half, tile)
            total = total + half[:, here, :] * col_sum(g_eta, tile)
            eta[:, here, :] = total * inverse[:, here, :]

    for f in range(FINE):
        nat_half[pl.ds(f, width, stride=FINE), :] = eta[f, pl.ds(0, width), :].T
    for block in range(blocks):
        eta_end[block] = nat_half[pl.ds(TILE + block * block_rows, block_rows), :]

    @pl.loop(1, columns)
    def _(shift):
        peer = column_at(shift)
        for rank in range(PAIR):
            send_out[PAIR * shift + rank] = eta_end[t_out[PAIR * peer + rank]]
        exchange(shift, send_out, recv_out, out_send, out_recv).start()

    for rank in range(PAIR):
        recv_out[PAIR * me + rank] = eta_end[t_out[PAIR * me + rank]]

    @pl.loop(1, columns)
    def _(shift):
        exchange(shift, send_out, recv_out, out_send, out_recv).wait()

    @pl.loop(0, slots)
    def _(slot):
        eta_next[0, slot] = recv_out[t_owner[slot]]


def solution(mesh):
    columns, bands = mesh.shape["bcol"], mesh.shape["brow"]

    def body(forcing, bottom_level, thickness, eta_prev, tropic_map):
        levels, rows, width = forcing.shape
        slots, block_rows = eta_prev.shape[1], eta_prev.shape[2]
        blocks = rows // block_rows
        sizes = (columns, bands, block_rows, rows, levels, slots, width)
        f32, dma = jnp.float32, pltpu.SemaphoreType.DMA

        def vmem(*shape):
            return pltpu.VMEM(shape, f32)

        def smem(*shape):
            return pltpu.SMEM(shape, jnp.int32)

        tall = width + TILE
        scratch = [
            pltpu.VMEM(forcing.shape, forcing.dtype),
            pltpu.VMEM((rows, width), jnp.int32),
            vmem(slots, block_rows, width),
        ]
        scratch += [vmem(PAIR * columns, block_rows, width)] * 4
        scratch += [vmem(blocks, block_rows, width)]
        scratch += [vmem(FINE * width, width)] * 3 + [vmem(width, width)]
        scratch += [vmem(FINE, tall, width)] * 7
        scratch += [vmem(FINE, tall + 2 * TILE, width)] * 2
        scratch += [vmem(2, FINE, TILE, width), vmem(FINE, TILE, width)]
        scratch += [vmem(2, 2, FINE, TILE, width), vmem(2, FINE, TILE, width)]
        scratch += [vmem(2, 2, TILE, width), vmem(6, 2, TILE, width), vmem(6, TILE, width)]
        scratch += [smem(*tropic_map.shape[::-1]), pltpu.SMEM((levels,), f32)]
        scratch += [
            smem(PAIR * columns), smem(blocks), smem(PAIR * columns), smem(slots), smem(blocks)
        ]
        scratch += [dma((blocks,))] + [dma] * 4 + [dma((columns,))] * 4 + [dma((16,))] * 2
        return pl.pallas_call(
            functools.partial(kernel, sizes),
            out_shape=jax.ShapeDtypeStruct(eta_prev.shape, f32),
            in_specs=[pl.BlockSpec(memory_space=pl.ANY)] * 5,
            out_specs=pl.BlockSpec(memory_space=pltpu.VMEM),
            scratch_shapes=scratch,
            compiler_params=pltpu.CompilerParams(
                collective_id=0, has_side_effects=True, vmem_limit_bytes=56 * 1024 * 1024
            ),
            cost_estimate=pl.CostEstimate(
                flops=60_000_000, bytes_accessed=18_000_000, transcendentals=0
            ),
        )(tropic_map.T, thickness, forcing, bottom_level, eta_prev)

    in_specs = (P(None, "brow", "bcol"), P("brow", "bcol"), P(), P("brow", "bcol", None, None), P())
    out_specs = P("brow", "bcol", None, None)
    return jax.shard_map(body, mesh=mesh, in_specs=in_specs, out_specs=out_specs, check_vma=False)
```

```python
import functools
import math

import jax
import jax.numpy as jnp
from jax import lax
from jax.experimental import pallas as pl
from jax.experimental.pallas import tpu as pltpu
from jax.sharding import PartitionSpec as P

MESH = pl.DeviceIdType.MESH
ITERS = 4
PAIR = 2
HALO = 4
TILE = 8
IN_ROWS = 40
OUT_ROW, OUT_ROWS = 4, 32
CHUNK = 128
FINE = 9
SURFACE = 0.25


def kernel(
    sizes,
    tropic_map, thickness, forcing, bottom_level, eta_prev,
    eta_next,
    forcing_v, bottom_v, prev_v,
    send_in_a, recv_in_a, send_in_b, recv_in_b,
    send_out_a, recv_out_a, send_out_b, recv_out_b,
    end_a, end_b,
    nat_half, nat_source, nat_eta, corner,
    raw, half, source, rhs, inverse, eta_a, eta_b, rest,
    g_eta, g_half,
    strip_first, col_first, strip_eta, col_eta,
    edge_first, row_first, row_eta,
    map_v, thick,
    t_in, t_clinic, t_out, t_owner, owner_of,
    load_sem, prev_sem, bottom_sem, map_sem, thick_sem,
    exchange_send, exchange_recv,
    halo_send, halo_recv,
):
    columns, bands, block_rows, rows, levels, slots, width = sizes
    blocks = rows // block_rows
    band = lax.axis_index("brow")
    me = lax.axis_index("bcol")
    base = me * slots
    first_row = band * blocks

    def column_at(shift):
        return lax.rem(me + shift + columns, columns)

    def band_at(shift):
        return lax.rem(band + shift + bands, bands)

    barrier = pltpu.get_barrier_semaphore()

    @pl.loop(1, columns)
    def _(shift):
        pl.semaphore_signal(barrier, inc=1, device_id=(band, column_at(shift)), device_id_type=MESH)

    beside = [(up, across) for up in (-1, 1) for across in (-1, 0, 1)]
    for up, across in beside:
        pl.semaphore_signal(
            barrier, inc=1, device_id=(band_at(up), column_at(across)), device_id_type=MESH
        )

    map_copy = pltpu.make_async_copy(tropic_map, map_v, map_sem)
    prev_copy = pltpu.make_async_copy(eta_prev.at[0], prev_v, prev_sem)
    thick_copy = pltpu.make_async_copy(thickness, thick, thick_sem)
    bottom_copy = pltpu.make_async_copy(bottom_level, bottom_v, bottom_sem)
    for copy in (map_copy, prev_copy, thick_copy, bottom_copy):
        copy.start()

    def load(block):
        span = pl.ds(pl.multiple_of(block * CHUNK, CHUNK), CHUNK)
        return pltpu.make_async_copy(
            forcing.at[:, span, :], forcing_v.at[:, span, :], load_sem.at[block]
        )

    @pl.loop(0, rows // CHUNK)
    def _(block):
        load(block).start()

    map_copy.wait()

    @pl.loop(0, columns)
    def _(column):
        first, second = jnp.int32(-1), jnp.int32(-1)
        for block in reversed(range(blocks)):
            slot = map_v[column, first_row + block] - base
            mine = (slot >= 0) & (slot < slots)
            second = jnp.where(mine, first, second)
            first = jnp.where(mine, slot, first)
        t_in[PAIR * column] = first
        t_in[PAIR * column + 1] = second

    prev_copy.wait()

    def gather_in(peer):
        for rank in range(PAIR):
            index = jnp.maximum(t_in[PAIR * peer + rank], 0)
            yield rank, prev_v[index]

    @pl.loop(1, columns)
    def _(shift):
        for rank, value in gather_in(column_at(shift)):
            send_in_a[PAIR * shift + rank] = value[:IN_ROWS]
            send_in_b[PAIR * shift + rank] = value[IN_ROWS:]

    for rank, value in gather_in(me):
        recv_in_a[PAIR * me + rank] = value[:IN_ROWS]
        recv_in_b[PAIR * me + rank] = value[IN_ROWS:]

    thick_copy.wait()
    bottom_copy.wait()
    table_lane = lax.broadcasted_iota(jnp.int32, (TILE, width), 1)
    depths = jnp.zeros((TILE, width), jnp.float32)
    for k in range(levels):
        depths = depths + jnp.where(table_lane > k, thick[k], 0.0)
    chunk_row = lax.broadcasted_iota(jnp.int32, (CHUNK, width), 0)

    def integrate(chunk):
        load(chunk).wait()
        start = pl.multiple_of(chunk * CHUNK, CHUNK)
        span = pl.ds(start, CHUNK)
        bottom = bottom_v[span, :]
        deepest = bottom.astype(jnp.float32).astype(jnp.bfloat16)

        def level(number, source_sum):
            for step in range(levels // 2):
                k = number * (levels // 2) + step
                mark = k.astype(jnp.float32).astype(jnp.bfloat16)
                layer = jnp.where(deepest > mark, forcing_v[k, span, :], jnp.bfloat16(0))
                source_sum = source_sum + thick[k] * layer.astype(jnp.float32)
            return source_sum

        zero = jnp.zeros((CHUNK, width), jnp.float32)
        source_sum = lax.fori_loop(0, 2, level, zero)
        depth_sum = jnp.concatenate(
            [
                jnp.take_along_axis(depths, bottom[at : at + TILE], axis=1)
                for at in range(0, CHUNK, TILE)
            ],
            axis=0,
        )
        wet = jnp.float32(0)
        for part in range(CHUNK // block_rows):
            block = chunk * (CHUNK // block_rows) + part
            here = jnp.where(map_v[me, first_row + block] >= 0, 1.0, 0.0)
            wet = jnp.where(chunk_row >= part * block_rows, here, wet)
        here = pl.ds(pl.multiple_of(TILE + start, TILE), CHUNK)
        nat_half[here, :] = depth_sum * (wet * (0.5 / levels)) + (wet - 1.0)
        nat_source[here, :] = source_sum * (wet * (1.0 / math.sqrt(levels)))

    pl.semaphore_wait(barrier, columns - 1 + len(beside))

    parts = (
        (send_in_a, recv_in_a), (send_in_b, recv_in_b),
        (send_out_a, recv_out_a), (send_out_b, recv_out_b),
    )

    def exchange(part, shift):
        sent, received = parts[part]
        return pltpu.make_async_remote_copy(
            src_ref=sent.at[pl.ds(PAIR * shift, PAIR)],
            dst_ref=received.at[pl.ds(PAIR * me, PAIR)],
            send_sem=exchange_send.at[part, shift],
            recv_sem=exchange_recv.at[part, shift],
            device_id=(band, column_at(shift)),
            device_id_type=MESH,
        )

    def start_all(part):
        @pl.loop(1, columns)
        def _(shift):
            exchange(part, shift).start()

    def wait_all(part):
        @pl.loop(1, columns)
        def _(shift):
            exchange(part, shift).wait()

    start_all(0)
    start_all(1)
    pl.loop(0, rows // CHUNK)(integrate)

    def remote(number, src, dst, device):
        return pltpu.make_async_remote_copy(
            src_ref=src,
            dst_ref=dst,
            send_sem=halo_send.at[number],
            recv_sem=halo_recv.at[number],
            device_id=device,
            device_id_type=MESH,
        )

    def row_copies(number, top, bottom, row):
        return [
            remote(
                number + place,
                top if up < 0 else bottom,
                row.at[place],
                (band_at(up), column_at(across)),
            )
            for place, (up, across) in enumerate(beside)
        ]

    def col_copies(number, to_left, to_right, col):
        return [
            remote(number + side, strip, col.at[side], (band, column_at(across)))
            for side, (strip, across) in enumerate(((to_left, -1), (to_right, 1)))
        ]

    has_above = jnp.where(band > 0, 1.0, 0.0)
    has_below = jnp.where(band < bands - 1, 1.0, 0.0)
    tile_lane = lax.broadcasted_iota(jnp.int32, (TILE, width), 1)
    low_lane = tile_lane < width // 2
    low_row = lax.broadcasted_iota(jnp.int32, (TILE, width), 0) < HALO
    low_rows = lax.broadcasted_iota(jnp.int32, (FINE, TILE, width), 1) < HALO
    above_at, below_at = 0, TILE + rows
    near = [(n, n) for n in range(TILE - HALO, TILE)]
    near += [(below_at + m, TILE + m) for m in range(HALO)]
    fine_near = sorted({n % FINE for n, _ in near})
    last = width - TILE
    side_rows = pl.ds(width, TILE)

    def turn(nat, field, fine):
        for f in fine:
            field[f, pl.ds(0, width), :] = nat[pl.ds(f, width, stride=FINE), :].T

    def ends_of(field):
        return field[:, pl.ds(0, TILE), :], field[:, pl.ds(last, TILE), :]

    def strip_of(field):
        return jnp.where(low_rows, *ends_of(field))

    def fill(nat, field, arrived_row, halo_columns, outside):
        for at, place, inside in ((above_at, 3, has_above), (below_at, 0, has_below)):
            right, middle, left = (arrived_row(place + k) for k in range(3))
            absent = (1.0 - inside) * outside
            nat[pl.ds(at, TILE), :] = middle * inside + absent
            side = jnp.where(low_lane, right, left) * inside + absent
            corner[pl.ds(TILE if at else 0, TILE), :] = side
        turn(nat, field, fine_near)
        turned = corner[...].T
        sides = jnp.where(low_row, turned[0:TILE, :], turned[last:width, :])
        field[:, side_rows, :] = halo_columns
        for n, lane in near:
            f, to = n % FINE, n // FINE
            moved = pltpu.roll(sides, (to - lane) % width, 1)
            field[f, side_rows, :] = jnp.where(tile_lane == to, moved, field[f, side_rows, :])

    corner[...] = jnp.zeros_like(corner)
    for number, nat in enumerate((nat_half, nat_source)):
        edge_first[0, number] = nat[pl.ds(TILE, TILE), :]
        edge_first[1, number] = nat[pl.ds(rows, TILE), :]
    first_rows = row_copies(0, edge_first.at[0], edge_first.at[1], row_first)
    for copy in first_rows:
        copy.start()
    turn(nat_half, raw, range(FINE))
    turn(nat_source, source, range(FINE))
    (raw_start, raw_end), (source_start, source_end) = ends_of(raw), ends_of(source)
    strip_first[0] = jnp.where(low_rows, raw_start, pltpu.roll(source_start, HALO, 1))
    strip_first[1] = jnp.where(low_rows, pltpu.roll(source_end, HALO, 1), raw_end)
    first_cols = col_copies(6, strip_first.at[0], strip_first.at[1], col_first)
    for copy in first_cols:
        copy.start()

    for block in range(blocks):
        value = map_v[me, first_row + block]
        owner_of[block] = jnp.where(value >= 0, value // slots, -1)
    for block in range(blocks):
        owner = owner_of[block]
        rank = jnp.int32(0)
        for before in range(block):
            rank = jnp.where(owner_of[before] == owner, 1, rank)
        t_clinic[block] = jnp.where(owner >= 0, owner * PAIR + rank, 0)

    @pl.loop(0, columns)
    def _(owner):
        first, second = jnp.int32(0), jnp.int32(0)
        for block in reversed(range(blocks)):
            mine = owner_of[block] == owner
            second = jnp.where(mine, first, second)
            first = jnp.where(mine, block, first)
        t_out[PAIR * owner] = first
        t_out[PAIR * owner + 1] = second

    @pl.loop(0, slots)
    def _(slot):
        place = jnp.int32(0)
        for entry in range(PAIR * columns):
            place = jnp.where(t_in[entry] == slot, entry, place)
        t_owner[slot] = place

    for copy in first_rows + first_cols:
        copy.wait()
    raw_halo = jnp.where(low_rows, col_first[0], col_first[1])
    source_halo = pltpu.roll(jnp.where(low_rows, col_first[1], col_first[0]), HALO, 1)
    fill(nat_half, raw, lambda p: row_first[p, 0], raw_halo, -1.0)
    fill(nat_source, source, lambda p: row_first[p, 1], source_halo, 0.0)

    tiles = width // TILE + 1

    def tile_at(tile):
        return pl.ds(TILE * tile, TILE)

    def row_sum(value):
        before = jnp.concatenate([pltpu.roll(value[FINE - 1 :], 1, 2), value[: FINE - 1]], axis=0)
        after = jnp.concatenate([value[1:], pltpu.roll(value[:1], width - 1, 2)], axis=0)
        return before + after

    def put(field, tile, value):
        field[:, tile_at(tile + 1), :] = value
        if tile == tiles - 1:
            field[:, tile_at(0), :] = value
        if tile == 0:
            field[:, tile_at(tiles + 1), :] = value

    def col_sum(field, tile):
        start = TILE * (tile + 1)
        return field[:, pl.ds(start - 1, TILE), :] + field[:, pl.ds(start + 1, TILE), :]

    for tile in range(tiles):
        value = jnp.maximum(raw[:, tile_at(tile), :], 0.0)
        half[:, tile_at(tile), :] = value
        around = row_sum(value)
        put(g_half, tile, value + 0.5 * around)
        rest[:, tile_at(tile), :] = (SURFACE + 8.0 * value) + around
    for tile in range(tiles):
        diagonal = rest[:, tile_at(tile), :] + col_sum(g_half, tile)
        wet = raw[:, tile_at(tile), :] >= 0.0
        inverse[:, tile_at(tile), :] = jnp.where(wet, 1.0 / diagonal, 0.0)

    def sweeps(eta):
        for tile in range(tiles):
            here = tile_at(tile)
            rhs[:, here, :] = (SURFACE + 2.0 * half[:, here, :]) * eta[:, here, :] + source[
                :, here, :
            ]

        @pl.loop(0, ITERS)
        def _(iteration):
            for tile in range(tiles):
                here = tile_at(tile)
                value, weight = eta[:, here, :], half[:, here, :]
                scaled = value * weight
                around, scaled_around = row_sum(value), row_sum(scaled)
                put(g_eta, tile, value + 0.5 * around)
                put(g_half, tile, scaled + 0.5 * scaled_around)
                rest[:, here, :] = rhs[:, here, :] + weight * around + scaled_around
            for tile in range(tiles):
                here = tile_at(tile)
                total = rest[:, here, :] + col_sum(g_half, tile)
                total = total + half[:, here, :] * col_sum(g_eta, tile)
                eta[:, here, :] = total * inverse[:, here, :]

        for f in range(FINE):
            nat_half[pl.ds(f, width, stride=FINE), :] = eta[f, pl.ds(0, width), :].T

    def unpack(part, received, at, count):
        wait_all(part)
        for block in range(blocks):
            wet = jnp.where(map_v[me, first_row + block] >= 0, 1.0, 0.0)
            there = pl.ds(TILE + block * block_rows + at, count)
            nat_eta[there, :] = received[t_clinic[block]] * wet

    def send_back(part, end):
        sent, received = parts[part]

        @pl.loop(1, columns)
        def _(shift):
            peer = column_at(shift)
            for rank in range(PAIR):
                sent[PAIR * shift + rank] = end[t_out[PAIR * peer + rank]]
            exchange(part, shift).start()

        for rank in range(PAIR):
            received[PAIR * me + rank] = end[t_out[PAIR * me + rank]]

    unpack(0, recv_in_a, 0, IN_ROWS)
    turn(nat_eta, eta_a, range(FINE))
    strip_eta[0] = strip_of(eta_a)
    cols_a = col_copies(8, strip_eta.at[0], strip_eta.at[0], col_eta.at[0])
    for copy in cols_a:
        copy.start()

    unpack(1, recv_in_b, IN_ROWS, block_rows - IN_ROWS)
    rows_b = row_copies(10, nat_eta.at[pl.ds(TILE, TILE)], nat_eta.at[pl.ds(rows, TILE)], row_eta)
    for copy in rows_b:
        copy.start()
    turn(nat_eta, eta_b, range(FINE))
    strip_eta[1] = strip_of(eta_b)
    cols_b = col_copies(16, strip_eta.at[1], strip_eta.at[1], col_eta.at[1])
    for copy in cols_b:
        copy.start()

    for copy in cols_a:
        copy.wait()
    eta_a[:, side_rows, :] = jnp.where(low_rows, col_eta[0, 0], col_eta[0, 1])
    sweeps(eta_a)
    for block in range(blocks):
        end_a[block] = nat_half[pl.ds(TILE + block * block_rows + OUT_ROW, OUT_ROWS), :]
    send_back(2, end_a)

    for copy in rows_b + cols_b:
        copy.wait()
    halo_b = jnp.where(low_rows, col_eta[1, 0], col_eta[1, 1])
    fill(nat_eta, eta_b, lambda p: row_eta[p], halo_b, 0.0)
    sweeps(eta_b)
    behind = block_rows - OUT_ROW - OUT_ROWS
    for block in range(blocks):
        start = TILE + block * block_rows
        end_b[block, pl.ds(0, behind), :] = nat_half[
            pl.ds(start + OUT_ROW + OUT_ROWS, behind), :
        ]
        end_b[block, pl.ds(behind, OUT_ROW), :] = nat_half[pl.ds(start, OUT_ROW), :]
    send_back(3, end_b)

    wait_all(2)

    @pl.loop(0, slots)
    def _(slot):
        eta_next[0, slot, pl.ds(OUT_ROW, OUT_ROWS), :] = recv_out_a[t_owner[slot]]

    wait_all(3)

    @pl.loop(0, slots)
    def _(slot):
        value = recv_out_b[t_owner[slot]]
        eta_next[0, slot, pl.ds(OUT_ROW + OUT_ROWS, behind), :] = value[:behind]
        eta_next[0, slot, pl.ds(0, OUT_ROW), :] = value[behind:]


def solution(mesh):
    columns, bands = mesh.shape["bcol"], mesh.shape["brow"]

    def body(forcing, bottom_level, thickness, eta_prev, tropic_map):
        levels, rows, width = forcing.shape
        slots, block_rows = eta_prev.shape[1], eta_prev.shape[2]
        blocks = rows // block_rows
        sizes = (columns, bands, block_rows, rows, levels, slots, width)
        f32, dma = jnp.float32, pltpu.SemaphoreType.DMA

        def vmem(*shape):
            return pltpu.VMEM(shape, f32)

        def smem(*shape):
            return pltpu.SMEM(shape, jnp.int32)

        tall = width + TILE
        scratch = [
            pltpu.VMEM(forcing.shape, forcing.dtype),
            pltpu.VMEM((rows, width), jnp.int32),
            vmem(slots, block_rows, width),
        ]
        for count in (IN_ROWS, block_rows - IN_ROWS, OUT_ROWS, block_rows - OUT_ROWS):
            scratch += [vmem(PAIR * columns, count, width)] * 2
        scratch += [vmem(blocks, OUT_ROWS, width), vmem(blocks, block_rows - OUT_ROWS, width)]
        scratch += [vmem(FINE * width, width)] * 3 + [vmem(width, width)]
        scratch += [vmem(FINE, tall, width)] * 8
        scratch += [vmem(FINE, tall + 2 * TILE, width)] * 2
        scratch += [vmem(2, FINE, TILE, width)] * 3 + [vmem(2, 2, FINE, TILE, width)]
        scratch += [vmem(2, 2, TILE, width), vmem(6, 2, TILE, width), vmem(6, TILE, width)]
        scratch += [smem(*tropic_map.shape[::-1]), pltpu.SMEM((levels,), f32)]
        scratch += [
            smem(PAIR * columns), smem(blocks), smem(PAIR * columns), smem(slots), smem(blocks)
        ]
        scratch += [dma((rows // CHUNK,))] + [dma] * 4 + [dma((4, columns))] * 2 + [dma((18,))] * 2
        return pl.pallas_call(
            functools.partial(kernel, sizes),
            out_shape=pltpu.VMEM(eta_prev.shape, f32),
            in_specs=[pl.BlockSpec(memory_space=pl.ANY)] * 5,
            out_specs=pl.BlockSpec(memory_space=pltpu.VMEM),
            scratch_shapes=scratch,
            compiler_params=pltpu.CompilerParams(
                collective_id=0, has_side_effects=True, vmem_limit_bytes=56 * 1024 * 1024
            ),
            cost_estimate=pl.CostEstimate(
                flops=60_000_000, bytes_accessed=18_000_000, transcendentals=0
            ),
        )(tropic_map.T, thickness, forcing, bottom_level, eta_prev)

    in_specs = (P(None, "brow", "bcol"), P("brow", "bcol"), P(), P("brow", "bcol", None, None), P())
    out_specs = P("brow", "bcol", None, None)
    return jax.shard_map(body, mesh=mesh, in_specs=in_specs, out_specs=out_specs, check_vma=False)
```

```python
import functools
import math

import jax
import jax.numpy as jnp
from jax import lax
from jax.experimental import pallas as pl
from jax.experimental.pallas import tpu as pltpu
from jax.sharding import PartitionSpec as P

MESH = pl.DeviceIdType.MESH
ITERS = 4
PAIR = 2
HALO = 4
TILE = 8
IN_ROWS = 40
OUT_ROW, OUT_ROWS = 4, 32
CHUNK = 128
FINE = 9
SURFACE = 0.25


def kernel(
    sizes,
    tropic_map, thickness, forcing, bottom_level, eta_prev,
    eta_next,
    forcing_v, bottom_v, prev_v,
    send_in_a, recv_in_a, send_in_b, recv_in_b,
    send_out_a, recv_out_a, send_out_b, recv_out_b,
    end_a, end_b,
    nat_half, nat_source, nat_eta, corner,
    raw, half, source, rhs, inverse, eta_a, eta_b, rest,
    g_eta, g_half,
    strip_first, col_first, strip_eta, col_eta,
    edge_first, row_first, row_eta,
    map_v, thick,
    t_in, t_clinic, t_out, t_owner, owner_of,
    load_sem, prev_sem, bottom_sem, map_sem, thick_sem,
    exchange_send, exchange_recv,
    halo_send, halo_recv,
):
    columns, bands, block_rows, rows, levels, slots, width = sizes
    blocks = rows // block_rows
    band = lax.axis_index("brow")
    me = lax.axis_index("bcol")
    base = me * slots
    first_row = band * blocks

    def column_at(shift):
        return lax.rem(me + shift + columns, columns)

    def band_at(shift):
        return lax.rem(band + shift + bands, bands)

    barrier = pltpu.get_barrier_semaphore()

    @pl.loop(1, columns)
    def _(shift):
        pl.semaphore_signal(barrier, inc=1, device_id=(band, column_at(shift)), device_id_type=MESH)

    beside = [(up, across) for up in (-1, 1) for across in (-1, 0, 1)]
    for up, across in beside:
        pl.semaphore_signal(
            barrier, inc=1, device_id=(band_at(up), column_at(across)), device_id_type=MESH
        )

    map_copy = pltpu.make_async_copy(tropic_map, map_v, map_sem)
    prev_copy = pltpu.make_async_copy(eta_prev.at[0], prev_v, prev_sem)
    thick_copy = pltpu.make_async_copy(thickness, thick, thick_sem)
    bottom_copy = pltpu.make_async_copy(bottom_level, bottom_v, bottom_sem)
    for copy in (map_copy, prev_copy, thick_copy, bottom_copy):
        copy.start()

    def load(block):
        span = pl.ds(pl.multiple_of(block * CHUNK, CHUNK), CHUNK)
        return pltpu.make_async_copy(
            forcing.at[:, span, :], forcing_v.at[:, span, :], load_sem.at[block]
        )

    @pl.loop(0, rows // CHUNK)
    def _(block):
        load(block).start()

    map_copy.wait()

    @pl.loop(0, columns)
    def _(column):
        first, second = jnp.int32(-1), jnp.int32(-1)
        for block in reversed(range(blocks)):
            slot = map_v[column, first_row + block] - base
            mine = (slot >= 0) & (slot < slots)
            second = jnp.where(mine, first, second)
            first = jnp.where(mine, slot, first)
        t_in[PAIR * column] = first
        t_in[PAIR * column + 1] = second

    prev_copy.wait()

    def gather_in(peer):
        for rank in range(PAIR):
            index = jnp.maximum(t_in[PAIR * peer + rank], 0)
            yield rank, prev_v[index]

    @pl.loop(1, columns)
    def _(shift):
        for rank, value in gather_in(column_at(shift)):
            send_in_a[PAIR * shift + rank] = value[:IN_ROWS]
            send_in_b[PAIR * shift + rank] = value[IN_ROWS:]

    for rank, value in gather_in(me):
        recv_in_a[PAIR * me + rank] = value[:IN_ROWS]
        recv_in_b[PAIR * me + rank] = value[IN_ROWS:]

    thick_copy.wait()
    bottom_copy.wait()
    table_lane = lax.broadcasted_iota(jnp.int32, (TILE, width), 1)
    depths = jnp.zeros((TILE, width), jnp.float32)
    for k in range(levels):
        depths = depths + jnp.where(table_lane > k, thick[k], 0.0)
    chunk_row = lax.broadcasted_iota(jnp.int32, (CHUNK, width), 0)

    def integrate(chunk):
        load(chunk).wait()
        start = pl.multiple_of(chunk * CHUNK, CHUNK)
        span = pl.ds(start, CHUNK)
        bottom = bottom_v[span, :]
        deepest = bottom.astype(jnp.float32).astype(jnp.bfloat16)

        def level(number, source_sum):
            for step in range(levels // 2):
                k = number * (levels // 2) + step
                mark = k.astype(jnp.float32).astype(jnp.bfloat16)
                layer = jnp.where(deepest > mark, forcing_v[k, span, :], jnp.bfloat16(0))
                source_sum = source_sum + thick[k] * layer.astype(jnp.float32)
            return source_sum

        zero = jnp.zeros((CHUNK, width), jnp.float32)
        source_sum = lax.fori_loop(0, 2, level, zero)
        depth_sum = jnp.concatenate(
            [
                jnp.take_along_axis(depths, bottom[at : at + TILE], axis=1)
                for at in range(0, CHUNK, TILE)
            ],
            axis=0,
        )
        wet = jnp.float32(0)
        for part in range(CHUNK // block_rows):
            block = chunk * (CHUNK // block_rows) + part
            here = jnp.where(map_v[me, first_row + block] >= 0, 1.0, 0.0)
            wet = jnp.where(chunk_row >= part * block_rows, here, wet)
        here = pl.ds(pl.multiple_of(TILE + start, TILE), CHUNK)
        nat_half[here, :] = depth_sum * (wet * (0.5 / levels)) + (wet - 1.0)
        nat_source[here, :] = source_sum * (wet * (1.0 / math.sqrt(levels)))

    pl.semaphore_wait(barrier, columns - 1 + len(beside))

    parts = (
        (send_in_a, recv_in_a), (send_in_b, recv_in_b),
        (send_out_a, recv_out_a), (send_out_b, recv_out_b),
    )

    def exchange(part, shift):
        sent, received = parts[part]
        return pltpu.make_async_remote_copy(
            src_ref=sent.at[pl.ds(PAIR * shift, PAIR)],
            dst_ref=received.at[pl.ds(PAIR * me, PAIR)],
            send_sem=exchange_send.at[part, shift],
            recv_sem=exchange_recv.at[part, shift],
            device_id=(band, column_at(shift)),
            device_id_type=MESH,
        )

    def start_all(part):
        @pl.loop(1, columns)
        def _(shift):
            exchange(part, shift).start()

    def wait_all(part):
        @pl.loop(1, columns)
        def _(shift):
            exchange(part, shift).wait()

    start_all(0)
    start_all(1)
    pl.loop(0, rows // CHUNK)(integrate)

    def remote(number, src, dst, device):
        return pltpu.make_async_remote_copy(
            src_ref=src,
            dst_ref=dst,
            send_sem=halo_send.at[number],
            recv_sem=halo_recv.at[number],
            device_id=device,
            device_id_type=MESH,
        )

    def row_copies(number, top, bottom, row):
        return [
            remote(
                number + place,
                top if up < 0 else bottom,
                row.at[place],
                (band_at(up), column_at(across)),
            )
            for place, (up, across) in enumerate(beside)
        ]

    def col_copies(number, to_left, to_right, col):
        return [
            remote(number + side, strip, col.at[side], (band, column_at(across)))
            for side, (strip, across) in enumerate(((to_left, -1), (to_right, 1)))
        ]

    has_above = jnp.where(band > 0, 1.0, 0.0)
    has_below = jnp.where(band < bands - 1, 1.0, 0.0)
    tile_lane = lax.broadcasted_iota(jnp.int32, (TILE, width), 1)
    low_lane = tile_lane < width // 2
    low_row = lax.broadcasted_iota(jnp.int32, (TILE, width), 0) < HALO
    low_rows = lax.broadcasted_iota(jnp.int32, (FINE, TILE, width), 1) < HALO
    above_at, below_at = 0, TILE + rows
    near = [(n, n) for n in range(TILE - HALO, TILE)]
    near += [(below_at + m, TILE + m) for m in range(HALO)]
    fine_near = sorted({n % FINE for n, _ in near})
    last = width - TILE
    side_rows = pl.ds(width, TILE)

    def turn(nat, field, fine):
        for f in fine:
            field[f, pl.ds(0, width), :] = nat[pl.ds(f, width, stride=FINE), :].T

    def ends_of(field):
        return field[:, pl.ds(0, TILE), :], field[:, pl.ds(last, TILE), :]

    def strip_of(field):
        return jnp.where(low_rows, *ends_of(field))

    def fill(nat, field, arrived_row, halo_columns, outside):
        for at, place, inside in ((above_at, 3, has_above), (below_at, 0, has_below)):
            right, middle, left = (arrived_row(place + k) for k in range(3))
            absent = (1.0 - inside) * outside
            nat[pl.ds(at, TILE), :] = middle * inside + absent
            side = jnp.where(low_lane, right, left) * inside + absent
            corner[pl.ds(TILE if at else 0, TILE), :] = side
        turn(nat, field, fine_near)
        turned = corner[...].T
        sides = jnp.where(low_row, turned[0:TILE, :], turned[last:width, :])
        field[:, side_rows, :] = halo_columns
        for n, lane in near:
            f, to = n % FINE, n // FINE
            moved = pltpu.roll(sides, (to - lane) % width, 1)
            field[f, side_rows, :] = jnp.where(tile_lane == to, moved, field[f, side_rows, :])

    corner[...] = jnp.zeros_like(corner)
    for number, nat in enumerate((nat_half, nat_source)):
        edge_first[0, number] = nat[pl.ds(TILE, TILE), :]
        edge_first[1, number] = nat[pl.ds(rows, TILE), :]
    first_rows = row_copies(0, edge_first.at[0], edge_first.at[1], row_first)
    for copy in first_rows:
        copy.start()
    turn(nat_half, raw, range(FINE))
    turn(nat_source, source, range(FINE))
    (raw_start, raw_end), (source_start, source_end) = ends_of(raw), ends_of(source)
    strip_first[0] = jnp.where(low_rows, raw_start, pltpu.roll(source_start, HALO, 1))
    strip_first[1] = jnp.where(low_rows, pltpu.roll(source_end, HALO, 1), raw_end)
    first_cols = col_copies(6, strip_first.at[0], strip_first.at[1], col_first)
    for copy in first_cols:
        copy.start()

    for block in range(blocks):
        value = map_v[me, first_row + block]
        owner_of[block] = jnp.where(value >= 0, value // slots, -1)
    for block in range(blocks):
        owner = owner_of[block]
        rank = jnp.int32(0)
        for before in range(block):
            rank = jnp.where(owner_of[before] == owner, 1, rank)
        t_clinic[block] = jnp.where(owner >= 0, owner * PAIR + rank, 0)

    @pl.loop(0, columns)
    def _(owner):
        first, second = jnp.int32(0), jnp.int32(0)
        for block in reversed(range(blocks)):
            mine = owner_of[block] == owner
            second = jnp.where(mine, first, second)
            first = jnp.where(mine, block, first)
        t_out[PAIR * owner] = first
        t_out[PAIR * owner + 1] = second

    @pl.loop(0, slots)
    def _(slot):
        place = jnp.int32(0)
        for entry in range(PAIR * columns):
            place = jnp.where(t_in[entry] == slot, entry, place)
        t_owner[slot] = place

    tiles = width // TILE + 1

    def tile_at(tile):
        return pl.ds(TILE * tile, TILE)

    def row_sum(value):
        before = jnp.concatenate([pltpu.roll(value[FINE - 1 :], 1, 2), value[: FINE - 1]], axis=0)
        after = jnp.concatenate([value[1:], pltpu.roll(value[:1], width - 1, 2)], axis=0)
        return before + after

    def put(field, tile, value):
        field[:, tile_at(tile + 1), :] = value
        if tile == tiles - 1:
            field[:, tile_at(0), :] = value
        if tile == 0:
            field[:, tile_at(tiles + 1), :] = value

    def col_sum(field, tile):
        start = TILE * (tile + 1)
        return field[:, pl.ds(start - 1, TILE), :] + field[:, pl.ds(start + 1, TILE), :]

    def sweeps(eta):
        for tile in range(tiles):
            here = tile_at(tile)
            rhs[:, here, :] = (SURFACE + 2.0 * half[:, here, :]) * eta[:, here, :] + source[
                :, here, :
            ]

        @pl.loop(0, ITERS)
        def _(iteration):
            for tile in range(tiles):
                here = tile_at(tile)
                value, weight = eta[:, here, :], half[:, here, :]
                scaled = value * weight
                around, scaled_around = row_sum(value), row_sum(scaled)
                put(g_eta, tile, value + 0.5 * around)
                put(g_half, tile, scaled + 0.5 * scaled_around)
                rest[:, here, :] = rhs[:, here, :] + weight * around + scaled_around
            for tile in range(tiles):
                here = tile_at(tile)
                total = rest[:, here, :] + col_sum(g_half, tile)
                total = total + half[:, here, :] * col_sum(g_eta, tile)
                eta[:, here, :] = total * inverse[:, here, :]

        for f in range(FINE):
            nat_half[pl.ds(f, width, stride=FINE), :] = eta[f, pl.ds(0, width), :].T

    def unpack(part, received, at, count):
        wait_all(part)
        for block in range(blocks):
            wet = jnp.where(map_v[me, first_row + block] >= 0, 1.0, 0.0)
            there = pl.ds(TILE + block * block_rows + at, count)
            nat_eta[there, :] = received[t_clinic[block]] * wet

    def send_back(part, end):
        sent, received = parts[part]

        @pl.loop(1, columns)
        def _(shift):
            peer = column_at(shift)
            for rank in range(PAIR):
                sent[PAIR * shift + rank] = end[t_out[PAIR * peer + rank]]
            exchange(part, shift).start()

        for rank in range(PAIR):
            received[PAIR * me + rank] = end[t_out[PAIR * me + rank]]

    unpack(0, recv_in_a, 0, IN_ROWS)
    turn(nat_eta, eta_a, range(FINE))
    strip_eta[0] = strip_of(eta_a)
    cols_a = col_copies(8, strip_eta.at[0], strip_eta.at[0], col_eta.at[0])
    for copy in cols_a:
        copy.start()


    unpack(1, recv_in_b, IN_ROWS, block_rows - IN_ROWS)
    rows_b = row_copies(10, nat_eta.at[pl.ds(TILE, TILE)], nat_eta.at[pl.ds(rows, TILE)], row_eta)
    for copy in rows_b:
        copy.start()
    turn(nat_eta, eta_b, range(FINE))
    strip_eta[1] = strip_of(eta_b)
    cols_b = col_copies(16, strip_eta.at[1], strip_eta.at[1], col_eta.at[1])
    for copy in cols_b:
        copy.start()

    for copy in first_rows + first_cols:
        copy.wait()
    raw_halo = jnp.where(low_rows, col_first[0], col_first[1])
    source_halo = pltpu.roll(jnp.where(low_rows, col_first[1], col_first[0]), HALO, 1)
    fill(nat_half, raw, lambda p: row_first[p, 0], raw_halo, -1.0)
    fill(nat_source, source, lambda p: row_first[p, 1], source_halo, 0.0)
    for tile in range(tiles):
        value = jnp.maximum(raw[:, tile_at(tile), :], 0.0)
        half[:, tile_at(tile), :] = value
        around = row_sum(value)
        put(g_half, tile, value + 0.5 * around)
        rest[:, tile_at(tile), :] = (SURFACE + 8.0 * value) + around
    for tile in range(tiles):
        diagonal = rest[:, tile_at(tile), :] + col_sum(g_half, tile)
        wet = raw[:, tile_at(tile), :] >= 0.0
        inverse[:, tile_at(tile), :] = jnp.where(wet, 1.0 / diagonal, 0.0)

    for copy in cols_a:
        copy.wait()
    eta_a[:, side_rows, :] = jnp.where(low_rows, col_eta[0, 0], col_eta[0, 1])
    sweeps(eta_a)
    for block in range(blocks):
        end_a[block] = nat_half[pl.ds(TILE + block * block_rows + OUT_ROW, OUT_ROWS), :]
    send_back(2, end_a)

    for copy in rows_b + cols_b:
        copy.wait()
    halo_b = jnp.where(low_rows, col_eta[1, 0], col_eta[1, 1])
    fill(nat_eta, eta_b, lambda p: row_eta[p], halo_b, 0.0)
    sweeps(eta_b)
    behind = block_rows - OUT_ROW - OUT_ROWS
    for block in range(blocks):
        start = TILE + block * block_rows
        end_b[block, pl.ds(0, behind), :] = nat_half[
            pl.ds(start + OUT_ROW + OUT_ROWS, behind), :
        ]
        end_b[block, pl.ds(behind, OUT_ROW), :] = nat_half[pl.ds(start, OUT_ROW), :]
    send_back(3, end_b)

    wait_all(2)

    @pl.loop(0, slots)
    def _(slot):
        eta_next[0, slot, pl.ds(OUT_ROW, OUT_ROWS), :] = recv_out_a[t_owner[slot]]

    wait_all(3)

    @pl.loop(0, slots)
    def _(slot):
        value = recv_out_b[t_owner[slot]]
        eta_next[0, slot, pl.ds(OUT_ROW + OUT_ROWS, behind), :] = value[:behind]
        eta_next[0, slot, pl.ds(0, OUT_ROW), :] = value[behind:]


def solution(mesh):
    columns, bands = mesh.shape["bcol"], mesh.shape["brow"]

    def body(forcing, bottom_level, thickness, eta_prev, tropic_map):
        levels, rows, width = forcing.shape
        slots, block_rows = eta_prev.shape[1], eta_prev.shape[2]
        blocks = rows // block_rows
        sizes = (columns, bands, block_rows, rows, levels, slots, width)
        f32, dma = jnp.float32, pltpu.SemaphoreType.DMA

        def vmem(*shape):
            return pltpu.VMEM(shape, f32)

        def smem(*shape):
            return pltpu.SMEM(shape, jnp.int32)

        tall = width + TILE
        scratch = [
            pltpu.VMEM(forcing.shape, forcing.dtype),
            pltpu.VMEM((rows, width), jnp.int32),
            vmem(slots, block_rows, width),
        ]
        for count in (IN_ROWS, block_rows - IN_ROWS, OUT_ROWS, block_rows - OUT_ROWS):
            scratch += [vmem(PAIR * columns, count, width)] * 2
        scratch += [vmem(blocks, OUT_ROWS, width), vmem(blocks, block_rows - OUT_ROWS, width)]
        scratch += [vmem(FINE * width, width)] * 3 + [vmem(width, width)]
        scratch += [vmem(FINE, tall, width)] * 8
        scratch += [vmem(FINE, tall + 2 * TILE, width)] * 2
        scratch += [vmem(2, FINE, TILE, width)] * 3 + [vmem(2, 2, FINE, TILE, width)]
        scratch += [vmem(2, 2, TILE, width), vmem(6, 2, TILE, width), vmem(6, TILE, width)]
        scratch += [smem(*tropic_map.shape[::-1]), pltpu.SMEM((levels,), f32)]
        scratch += [
            smem(PAIR * columns), smem(blocks), smem(PAIR * columns), smem(slots), smem(blocks)
        ]
        scratch += [dma((rows // CHUNK,))] + [dma] * 4 + [dma((4, columns))] * 2 + [dma((18,))] * 2
        return pl.pallas_call(
            functools.partial(kernel, sizes),
            out_shape=pltpu.VMEM(eta_prev.shape, f32),
            in_specs=[pl.BlockSpec(memory_space=pl.ANY)] * 5,
            out_specs=pl.BlockSpec(memory_space=pltpu.VMEM),
            scratch_shapes=scratch,
            compiler_params=pltpu.CompilerParams(
                collective_id=0, has_side_effects=True, vmem_limit_bytes=56 * 1024 * 1024
            ),
            cost_estimate=pl.CostEstimate(
                flops=60_000_000, bytes_accessed=18_000_000, transcendentals=0
            ),
        )(tropic_map.T, thickness, forcing, bottom_level, eta_prev)

    in_specs = (P(None, "brow", "bcol"), P("brow", "bcol"), P(), P("brow", "bcol", None, None), P())
    out_specs = P("brow", "bcol", None, None)
    return jax.shard_map(body, mesh=mesh, in_specs=in_specs, out_specs=out_specs, check_vma=False)
```

```python
import functools
import math

import jax
import jax.numpy as jnp
from jax import lax
from jax.experimental import pallas as pl
from jax.experimental.pallas import tpu as pltpu
from jax.sharding import PartitionSpec as P

MESH = pl.DeviceIdType.MESH
ITERS = 4
PAIR = 2
HALO = 4
TILE = 8
IN_ROWS = 40
OUT_ROW, OUT_ROWS = 4, 32
CHUNK = 128
FINE = 9
SURFACE = 0.25


def kernel(
    sizes,
    tropic_map, thickness, forcing, bottom_level, eta_prev,
    eta_next,
    forcing_v, bottom_v, prev_v,
    send_in_a, recv_in_a, send_in_b, recv_in_b,
    send_out_a, recv_out_a, send_out_b, recv_out_b,
    end_a, end_b,
    nat_half, nat_source, nat_eta, corner,
    raw, half, source, rhs, inverse, eta_a, eta_b, rest,
    g_eta, g_half,
    strip_first, col_first, strip_eta, col_eta,
    edge_first, row_first, row_eta,
    map_v, thick,
    t_in, t_clinic, t_out, t_owner, owner_of,
    load_sem, prev_sem, bottom_sem, map_sem, thick_sem,
    exchange_send, exchange_recv,
    halo_send, halo_recv,
):
    columns, bands, block_rows, rows, levels, slots, width = sizes
    blocks = rows // block_rows
    band = lax.axis_index("brow")
    me = lax.axis_index("bcol")
    base = me * slots
    first_row = band * blocks

    def column_at(shift):
        return lax.rem(me + shift + columns, columns)

    def band_at(shift):
        return lax.rem(band + shift + bands, bands)

    barrier = pltpu.get_barrier_semaphore()

    @pl.loop(1, columns)
    def _(shift):
        pl.semaphore_signal(barrier, inc=1, device_id=(band, column_at(shift)), device_id_type=MESH)

    beside = [(up, across) for up in (-1, 1) for across in (-1, 0, 1)]
    for up, across in beside:
        pl.semaphore_signal(
            barrier, inc=1, device_id=(band_at(up), column_at(across)), device_id_type=MESH
        )

    map_copy = pltpu.make_async_copy(tropic_map, map_v, map_sem)
    prev_copy = pltpu.make_async_copy(eta_prev.at[0], prev_v, prev_sem)
    thick_copy = pltpu.make_async_copy(thickness, thick, thick_sem)
    bottom_copy = pltpu.make_async_copy(bottom_level, bottom_v, bottom_sem)
    for copy in (map_copy, prev_copy, thick_copy, bottom_copy):
        copy.start()

    def load(block):
        span = pl.ds(pl.multiple_of(block * CHUNK, CHUNK), CHUNK)
        return pltpu.make_async_copy(
            forcing.at[:, span, :], forcing_v.at[:, span, :], load_sem.at[block]
        )

    chunks = rows // CHUNK
    load(0).start()
    load(chunks - 1).start()

    @pl.loop(1, chunks - 1)
    def _(chunk):
        load(chunk).start()

    map_copy.wait()

    @pl.loop(0, columns)
    def _(column):
        first, second = jnp.int32(-1), jnp.int32(-1)
        for block in reversed(range(blocks)):
            slot = map_v[column, first_row + block] - base
            mine = (slot >= 0) & (slot < slots)
            second = jnp.where(mine, first, second)
            first = jnp.where(mine, slot, first)
        t_in[PAIR * column] = first
        t_in[PAIR * column + 1] = second

    prev_copy.wait()

    def gather_in(peer):
        for rank in range(PAIR):
            index = jnp.maximum(t_in[PAIR * peer + rank], 0)
            yield rank, prev_v[index]

    @pl.loop(1, columns)
    def _(shift):
        for rank, value in gather_in(column_at(shift)):
            send_in_a[PAIR * shift + rank] = value[:IN_ROWS]
            send_in_b[PAIR * shift + rank] = value[IN_ROWS:]

    for rank, value in gather_in(me):
        recv_in_a[PAIR * me + rank] = value[:IN_ROWS]
        recv_in_b[PAIR * me + rank] = value[IN_ROWS:]

    thick_copy.wait()
    bottom_copy.wait()
    table_lane = lax.broadcasted_iota(jnp.int32, (TILE, width), 1)
    depths = jnp.zeros((TILE, width), jnp.float32)
    for k in range(levels):
        depths = depths + jnp.where(table_lane > k, thick[k], 0.0)
    chunk_row = lax.broadcasted_iota(jnp.int32, (CHUNK, width), 0)

    def integrate(chunk):
        load(chunk).wait()
        start = pl.multiple_of(chunk * CHUNK, CHUNK)
        span = pl.ds(start, CHUNK)
        bottom = bottom_v[span, :]
        deepest = bottom.astype(jnp.float32).astype(jnp.bfloat16)

        def level(number, source_sum):
            for step in range(levels // 2):
                k = number * (levels // 2) + step
                mark = k.astype(jnp.float32).astype(jnp.bfloat16)
                layer = jnp.where(deepest > mark, forcing_v[k, span, :], jnp.bfloat16(0))
                source_sum = source_sum + thick[k] * layer.astype(jnp.float32)
            return source_sum

        zero = jnp.zeros((CHUNK, width), jnp.float32)
        source_sum = lax.fori_loop(0, 2, level, zero)
        depth_sum = jnp.concatenate(
            [
                jnp.take_along_axis(depths, bottom[at : at + TILE], axis=1)
                for at in range(0, CHUNK, TILE)
            ],
            axis=0,
        )
        wet = jnp.float32(0)
        for part in range(CHUNK // block_rows):
            block = chunk * (CHUNK // block_rows) + part
            here = jnp.where(map_v[me, first_row + block] >= 0, 1.0, 0.0)
            wet = jnp.where(chunk_row >= part * block_rows, here, wet)
        here = pl.ds(pl.multiple_of(TILE + start, TILE), CHUNK)
        nat_half[here, :] = depth_sum * (wet * (0.5 / levels)) + (wet - 1.0)
        nat_source[here, :] = source_sum * (wet * (1.0 / math.sqrt(levels)))

    pl.semaphore_wait(barrier, columns - 1 + len(beside))

    parts = (
        (send_in_a, recv_in_a), (send_in_b, recv_in_b),
        (send_out_a, recv_out_a), (send_out_b, recv_out_b),
    )

    def exchange(part, shift):
        sent, received = parts[part]
        return pltpu.make_async_remote_copy(
            src_ref=sent.at[pl.ds(PAIR * shift, PAIR)],
            dst_ref=received.at[pl.ds(PAIR * me, PAIR)],
            send_sem=exchange_send.at[part, shift],
            recv_sem=exchange_recv.at[part, shift],
            device_id=(band, column_at(shift)),
            device_id_type=MESH,
        )

    def start_all(part):
        @pl.loop(1, columns)
        def _(shift):
            exchange(part, shift).start()

    def wait_all(part):
        @pl.loop(1, columns)
        def _(shift):
            exchange(part, shift).wait()

    start_all(0)
    start_all(1)
    def remote(number, src, dst, device):
        return pltpu.make_async_remote_copy(
            src_ref=src,
            dst_ref=dst,
            send_sem=halo_send.at[number],
            recv_sem=halo_recv.at[number],
            device_id=device,
            device_id_type=MESH,
        )

    def row_copies(number, top, bottom, row):
        return [
            remote(
                number + place,
                top if up < 0 else bottom,
                row.at[place],
                (band_at(up), column_at(across)),
            )
            for place, (up, across) in enumerate(beside)
        ]

    def col_copies(number, to_left, to_right, col):
        return [
            remote(number + side, strip, col.at[side], (band, column_at(across)))
            for side, (strip, across) in enumerate(((to_left, -1), (to_right, 1)))
        ]

    has_above = jnp.where(band > 0, 1.0, 0.0)
    has_below = jnp.where(band < bands - 1, 1.0, 0.0)
    tile_lane = lax.broadcasted_iota(jnp.int32, (TILE, width), 1)
    low_lane = tile_lane < width // 2
    low_row = lax.broadcasted_iota(jnp.int32, (TILE, width), 0) < HALO
    low_rows = lax.broadcasted_iota(jnp.int32, (FINE, TILE, width), 1) < HALO
    above_at, below_at = 0, TILE + rows
    near = [(n, n) for n in range(TILE - HALO, TILE)]
    near += [(below_at + m, TILE + m) for m in range(HALO)]
    fine_near = sorted({n % FINE for n, _ in near})
    last = width - TILE
    side_rows = pl.ds(width, TILE)

    def turn(nat, field, fine):
        for f in fine:
            field[f, pl.ds(0, width), :] = nat[pl.ds(f, width, stride=FINE), :].T

    def ends_of(field):
        return field[:, pl.ds(0, TILE), :], field[:, pl.ds(last, TILE), :]

    def strip_of(field):
        return jnp.where(low_rows, *ends_of(field))

    def fill(nat, field, arrived_row, halo_columns, outside):
        for at, place, inside in ((above_at, 3, has_above), (below_at, 0, has_below)):
            right, middle, left = (arrived_row(place + k) for k in range(3))
            absent = (1.0 - inside) * outside
            nat[pl.ds(at, TILE), :] = middle * inside + absent
            side = jnp.where(low_lane, right, left) * inside + absent
            corner[pl.ds(TILE if at else 0, TILE), :] = side
        turn(nat, field, fine_near)
        turned = corner[...].T
        sides = jnp.where(low_row, turned[0:TILE, :], turned[last:width, :])
        field[:, side_rows, :] = halo_columns
        for n, lane in near:
            f, to = n % FINE, n // FINE
            moved = pltpu.roll(sides, (to - lane) % width, 1)
            field[f, side_rows, :] = jnp.where(tile_lane == to, moved, field[f, side_rows, :])

    pl.loop(0, 2)(lambda end: integrate(end * (chunks - 1)))
    corner[...] = jnp.zeros_like(corner)
    for number, nat in enumerate((nat_half, nat_source)):
        edge_first[0, number] = nat[pl.ds(TILE, TILE), :]
        edge_first[1, number] = nat[pl.ds(rows, TILE), :]
    first_rows = row_copies(0, edge_first.at[0], edge_first.at[1], row_first)
    for copy in first_rows:
        copy.start()
    pl.loop(1, chunks - 1)(integrate)
    turn(nat_half, raw, range(FINE))
    turn(nat_source, source, range(FINE))
    (raw_start, raw_end), (source_start, source_end) = ends_of(raw), ends_of(source)
    strip_first[0] = jnp.where(low_rows, raw_start, pltpu.roll(source_start, HALO, 1))
    strip_first[1] = jnp.where(low_rows, pltpu.roll(source_end, HALO, 1), raw_end)
    first_cols = col_copies(6, strip_first.at[0], strip_first.at[1], col_first)
    for copy in first_cols:
        copy.start()

    for block in range(blocks):
        value = map_v[me, first_row + block]
        owner_of[block] = jnp.where(value >= 0, value // slots, -1)
    for block in range(blocks):
        owner = owner_of[block]
        rank = jnp.int32(0)
        for before in range(block):
            rank = jnp.where(owner_of[before] == owner, 1, rank)
        t_clinic[block] = jnp.where(owner >= 0, owner * PAIR + rank, 0)

    @pl.loop(0, columns)
    def _(owner):
        first, second = jnp.int32(0), jnp.int32(0)
        for block in reversed(range(blocks)):
            mine = owner_of[block] == owner
            second = jnp.where(mine, first, second)
            first = jnp.where(mine, block, first)
        t_out[PAIR * owner] = first
        t_out[PAIR * owner + 1] = second

    @pl.loop(0, slots)
    def _(slot):
        place = jnp.int32(0)
        for entry in range(PAIR * columns):
            place = jnp.where(t_in[entry] == slot, entry, place)
        t_owner[slot] = place

    tiles = width // TILE + 1

    def tile_at(tile):
        return pl.ds(TILE * tile, TILE)

    def row_sum(value):
        before = jnp.concatenate([pltpu.roll(value[FINE - 1 :], 1, 2), value[: FINE - 1]], axis=0)
        after = jnp.concatenate([value[1:], pltpu.roll(value[:1], width - 1, 2)], axis=0)
        return before + after

    def put(field, tile, value):
        field[:, tile_at(tile + 1), :] = value
        if tile == tiles - 1:
            field[:, tile_at(0), :] = value
        if tile == 0:
            field[:, tile_at(tiles + 1), :] = value

    def col_sum(field, tile):
        start = TILE * (tile + 1)
        return field[:, pl.ds(start - 1, TILE), :] + field[:, pl.ds(start + 1, TILE), :]

    def sweeps(eta):
        for tile in range(tiles):
            here = tile_at(tile)
            rhs[:, here, :] = (SURFACE + 2.0 * half[:, here, :]) * eta[:, here, :] + source[
                :, here, :
            ]

        @pl.loop(0, ITERS)
        def _(iteration):
            for tile in range(tiles):
                here = tile_at(tile)
                value, weight = eta[:, here, :], half[:, here, :]
                scaled = value * weight
                around, scaled_around = row_sum(value), row_sum(scaled)
                put(g_eta, tile, value + 0.5 * around)
                put(g_half, tile, scaled + 0.5 * scaled_around)
                rest[:, here, :] = rhs[:, here, :] + weight * around + scaled_around
            for tile in range(tiles):
                here = tile_at(tile)
                total = rest[:, here, :] + col_sum(g_half, tile)
                total = total + half[:, here, :] * col_sum(g_eta, tile)
                eta[:, here, :] = total * inverse[:, here, :]

        for f in range(FINE):
            nat_half[pl.ds(f, width, stride=FINE), :] = eta[f, pl.ds(0, width), :].T

    def unpack(part, received, at, count):
        wait_all(part)
        for block in range(blocks):
            wet = jnp.where(map_v[me, first_row + block] >= 0, 1.0, 0.0)
            there = pl.ds(TILE + block * block_rows + at, count)
            nat_eta[there, :] = received[t_clinic[block]] * wet

    def send_back(part, end):
        sent, received = parts[part]

        @pl.loop(1, columns)
        def _(shift):
            peer = column_at(shift)
            for rank in range(PAIR):
                sent[PAIR * shift + rank] = end[t_out[PAIR * peer + rank]]
            exchange(part, shift).start()

        for rank in range(PAIR):
            received[PAIR * me + rank] = end[t_out[PAIR * me + rank]]

    unpack(0, recv_in_a, 0, IN_ROWS)
    turn(nat_eta, eta_a, range(FINE))
    strip_eta[0] = strip_of(eta_a)
    cols_a = col_copies(8, strip_eta.at[0], strip_eta.at[0], col_eta.at[0])
    for copy in cols_a:
        copy.start()


    unpack(1, recv_in_b, IN_ROWS, block_rows - IN_ROWS)
    rows_b = row_copies(10, nat_eta.at[pl.ds(TILE, TILE)], nat_eta.at[pl.ds(rows, TILE)], row_eta)
    for copy in rows_b:
        copy.start()
    turn(nat_eta, eta_b, range(FINE))
    strip_eta[1] = strip_of(eta_b)
    cols_b = col_copies(16, strip_eta.at[1], strip_eta.at[1], col_eta.at[1])
    for copy in cols_b:
        copy.start()

    for copy in first_rows + first_cols:
        copy.wait()
    raw_halo = jnp.where(low_rows, col_first[0], col_first[1])
    source_halo = pltpu.roll(jnp.where(low_rows, col_first[1], col_first[0]), HALO, 1)
    fill(nat_half, raw, lambda p: row_first[p, 0], raw_halo, -1.0)
    fill(nat_source, source, lambda p: row_first[p, 1], source_halo, 0.0)
    for tile in range(tiles):
        value = jnp.maximum(raw[:, tile_at(tile), :], 0.0)
        half[:, tile_at(tile), :] = value
        around = row_sum(value)
        put(g_half, tile, value + 0.5 * around)
        rest[:, tile_at(tile), :] = (SURFACE + 8.0 * value) + around
    for tile in range(tiles):
        diagonal = rest[:, tile_at(tile), :] + col_sum(g_half, tile)
        wet = raw[:, tile_at(tile), :] >= 0.0
        inverse[:, tile_at(tile), :] = jnp.where(wet, 1.0 / diagonal, 0.0)

    for copy in cols_a:
        copy.wait()
    eta_a[:, side_rows, :] = jnp.where(low_rows, col_eta[0, 0], col_eta[0, 1])
    sweeps(eta_a)
    for block in range(blocks):
        end_a[block] = nat_half[pl.ds(TILE + block * block_rows + OUT_ROW, OUT_ROWS), :]
    send_back(2, end_a)

    for copy in rows_b + cols_b:
        copy.wait()
    halo_b = jnp.where(low_rows, col_eta[1, 0], col_eta[1, 1])
    fill(nat_eta, eta_b, lambda p: row_eta[p], halo_b, 0.0)
    sweeps(eta_b)
    behind = block_rows - OUT_ROW - OUT_ROWS
    for block in range(blocks):
        start = TILE + block * block_rows
        end_b[block, pl.ds(0, behind), :] = nat_half[
            pl.ds(start + OUT_ROW + OUT_ROWS, behind), :
        ]
        end_b[block, pl.ds(behind, OUT_ROW), :] = nat_half[pl.ds(start, OUT_ROW), :]
    send_back(3, end_b)

    wait_all(2)

    @pl.loop(0, slots)
    def _(slot):
        eta_next[0, slot, pl.ds(OUT_ROW, OUT_ROWS), :] = recv_out_a[t_owner[slot]]

    wait_all(3)

    @pl.loop(0, slots)
    def _(slot):
        value = recv_out_b[t_owner[slot]]
        eta_next[0, slot, pl.ds(OUT_ROW + OUT_ROWS, behind), :] = value[:behind]
        eta_next[0, slot, pl.ds(0, OUT_ROW), :] = value[behind:]


def solution(mesh):
    columns, bands = mesh.shape["bcol"], mesh.shape["brow"]

    def body(forcing, bottom_level, thickness, eta_prev, tropic_map):
        levels, rows, width = forcing.shape
        slots, block_rows = eta_prev.shape[1], eta_prev.shape[2]
        blocks = rows // block_rows
        sizes = (columns, bands, block_rows, rows, levels, slots, width)
        f32, dma = jnp.float32, pltpu.SemaphoreType.DMA

        def vmem(*shape):
            return pltpu.VMEM(shape, f32)

        def smem(*shape):
            return pltpu.SMEM(shape, jnp.int32)

        tall = width + TILE
        scratch = [
            pltpu.VMEM(forcing.shape, forcing.dtype),
            pltpu.VMEM((rows, width), jnp.int32),
            vmem(slots, block_rows, width),
        ]
        for count in (IN_ROWS, block_rows - IN_ROWS, OUT_ROWS, block_rows - OUT_ROWS):
            scratch += [vmem(PAIR * columns, count, width)] * 2
        scratch += [vmem(blocks, OUT_ROWS, width), vmem(blocks, block_rows - OUT_ROWS, width)]
        scratch += [vmem(FINE * width, width)] * 3 + [vmem(width, width)]
        scratch += [vmem(FINE, tall, width)] * 8
        scratch += [vmem(FINE, tall + 2 * TILE, width)] * 2
        scratch += [vmem(2, FINE, TILE, width)] * 3 + [vmem(2, 2, FINE, TILE, width)]
        scratch += [vmem(2, 2, TILE, width), vmem(6, 2, TILE, width), vmem(6, TILE, width)]
        scratch += [smem(*tropic_map.shape[::-1]), pltpu.SMEM((levels,), f32)]
        scratch += [
            smem(PAIR * columns), smem(blocks), smem(PAIR * columns), smem(slots), smem(blocks)
        ]
        scratch += [dma((rows // CHUNK,))] + [dma] * 4 + [dma((4, columns))] * 2 + [dma((18,))] * 2
        return pl.pallas_call(
            functools.partial(kernel, sizes),
            out_shape=pltpu.VMEM(eta_prev.shape, f32),
            in_specs=[pl.BlockSpec(memory_space=pl.ANY)] * 5,
            out_specs=pl.BlockSpec(memory_space=pltpu.VMEM),
            scratch_shapes=scratch,
            compiler_params=pltpu.CompilerParams(
                collective_id=0, has_side_effects=True, vmem_limit_bytes=56 * 1024 * 1024
            ),
            cost_estimate=pl.CostEstimate(
                flops=60_000_000, bytes_accessed=18_000_000, transcendentals=0
            ),
        )(tropic_map.T, thickness, forcing, bottom_level, eta_prev)

    in_specs = (P(None, "brow", "bcol"), P("brow", "bcol"), P(), P("brow", "bcol", None, None), P())
    out_specs = P("brow", "bcol", None, None)
    return jax.shard_map(body, mesh=mesh, in_specs=in_specs, out_specs=out_specs, check_vma=False)
```

```python
import functools
import math

import jax
import jax.numpy as jnp
from jax import lax
from jax.experimental import pallas as pl
from jax.experimental.pallas import tpu as pltpu
from jax.sharding import PartitionSpec as P

MESH = pl.DeviceIdType.MESH
ITERS = 4
PAIR = 2
HALO = 4
TILE = 8
IN_ROWS = 40
OUT_ROW, OUT_ROWS = 4, 32
CHUNK = 128
FINE = 9
SURFACE = 0.25


def kernel(
    sizes,
    tropic_map, thickness, forcing, bottom_level, eta_prev,
    eta_next,
    forcing_v, bottom_v, prev_v,
    send_in_a, recv_in_a, send_in_b, recv_in_b,
    send_out_a, recv_out_a, send_out_b, recv_out_b,
    end_a, end_b,
    nat_half, nat_source, nat_eta, corner,
    raw, half, source, rhs, inverse, eta_a, eta_b, rest,
    g_eta, g_half,
    strip_first, col_first, strip_eta, col_eta,
    edge_first, row_first, row_eta,
    map_v, thick,
    t_in, t_clinic, t_out, t_owner, owner_of,
    load_sem, prev_sem, bottom_sem, map_sem, thick_sem,
    exchange_send, exchange_recv,
    halo_send, halo_recv,
):
    columns, bands, block_rows, rows, levels, slots, width = sizes
    blocks = rows // block_rows
    band = lax.axis_index("brow")
    me = lax.axis_index("bcol")
    base = me * slots
    first_row = band * blocks

    def column_at(shift):
        return lax.rem(me + shift + columns, columns)

    def band_at(shift):
        return lax.rem(band + shift + bands, bands)

    barrier = pltpu.get_barrier_semaphore()

    @pl.loop(1, columns)
    def _(shift):
        pl.semaphore_signal(barrier, inc=1, device_id=(band, column_at(shift)), device_id_type=MESH)

    beside = [(up, across) for up in (-1, 1) for across in (-1, 0, 1)]
    for up, across in beside:
        pl.semaphore_signal(
            barrier, inc=1, device_id=(band_at(up), column_at(across)), device_id_type=MESH
        )

    map_copy = pltpu.make_async_copy(tropic_map, map_v, map_sem)
    prev_copy = pltpu.make_async_copy(eta_prev.at[0], prev_v, prev_sem)
    thick_copy = pltpu.make_async_copy(thickness, thick, thick_sem)
    bottom_copy = pltpu.make_async_copy(bottom_level, bottom_v, bottom_sem)
    for copy in (map_copy, prev_copy, thick_copy, bottom_copy):
        copy.start()

    def load(block):
        span = pl.ds(pl.multiple_of(block * CHUNK, CHUNK), CHUNK)
        return pltpu.make_async_copy(
            forcing.at[:, span, :], forcing_v.at[:, span, :], load_sem.at[block]
        )

    chunks = rows // CHUNK
    load(0).start()
    load(chunks - 1).start()

    @pl.loop(1, chunks - 1)
    def _(chunk):
        load(chunk).start()

    map_copy.wait()

    @pl.loop(0, columns)
    def _(column):
        first, second = jnp.int32(-1), jnp.int32(-1)
        for block in reversed(range(blocks)):
            slot = map_v[column, first_row + block] - base
            mine = (slot >= 0) & (slot < slots)
            second = jnp.where(mine, first, second)
            first = jnp.where(mine, slot, first)
        t_in[PAIR * column] = first
        t_in[PAIR * column + 1] = second

    prev_copy.wait()

    def gather_in(peer):
        for rank in range(PAIR):
            index = jnp.maximum(t_in[PAIR * peer + rank], 0)
            yield rank, prev_v[index]

    @pl.loop(1, columns)
    def _(shift):
        for rank, value in gather_in(column_at(shift)):
            send_in_a[PAIR * shift + rank] = value[:IN_ROWS]
            send_in_b[PAIR * shift + rank] = value[IN_ROWS:]

    for rank, value in gather_in(me):
        recv_in_a[PAIR * me + rank] = value[:IN_ROWS]
        recv_in_b[PAIR * me + rank] = value[IN_ROWS:]

    thick_copy.wait()
    bottom_copy.wait()
    table_lane = lax.broadcasted_iota(jnp.int32, (TILE, width), 1)
    depths = jnp.zeros((TILE, width), jnp.float32)
    for k in range(levels):
        depths = depths + jnp.where(table_lane > k, thick[k], 0.0)
    chunk_row = lax.broadcasted_iota(jnp.int32, (CHUNK, width), 0)

    def integrate(chunk):
        load(chunk).wait()
        start = pl.multiple_of(chunk * CHUNK, CHUNK)
        span = pl.ds(start, CHUNK)
        bottom = bottom_v[span, :]
        deepest = bottom.astype(jnp.float32).astype(jnp.bfloat16)

        def level(number, source_sum):
            for step in range(levels // 2):
                k = number * (levels // 2) + step
                mark = k.astype(jnp.float32).astype(jnp.bfloat16)
                layer = jnp.where(deepest > mark, forcing_v[k, span, :], jnp.bfloat16(0))
                source_sum = source_sum + thick[k] * layer.astype(jnp.float32)
            return source_sum

        zero = jnp.zeros((CHUNK, width), jnp.float32)
        source_sum = lax.fori_loop(0, 2, level, zero)
        depth_sum = jnp.concatenate(
            [
                jnp.take_along_axis(depths, bottom[at : at + TILE], axis=1)
                for at in range(0, CHUNK, TILE)
            ],
            axis=0,
        )
        wet = jnp.float32(0)
        for part in range(CHUNK // block_rows):
            block = chunk * (CHUNK // block_rows) + part
            here = jnp.where(map_v[me, first_row + block] >= 0, 1.0, 0.0)
            wet = jnp.where(chunk_row >= part * block_rows, here, wet)
        here = pl.ds(pl.multiple_of(TILE + start, TILE), CHUNK)
        nat_half[here, :] = depth_sum * (wet * (0.5 / levels)) + (wet - 1.0)
        nat_source[here, :] = source_sum * (wet * (1.0 / math.sqrt(levels)))

    pl.semaphore_wait(barrier, columns - 1 + len(beside))

    parts = (
        (send_in_a, recv_in_a), (send_in_b, recv_in_b),
        (send_out_a, recv_out_a), (send_out_b, recv_out_b),
    )

    def exchange(part, shift):
        sent, received = parts[part]
        return pltpu.make_async_remote_copy(
            src_ref=sent.at[pl.ds(PAIR * shift, PAIR)],
            dst_ref=received.at[pl.ds(PAIR * me, PAIR)],
            send_sem=exchange_send.at[part, shift],
            recv_sem=exchange_recv.at[part, shift],
            device_id=(band, column_at(shift)),
            device_id_type=MESH,
        )

    def start_all(part):
        @pl.loop(1, columns)
        def _(shift):
            exchange(part, shift).start()

    def wait_all(part):
        @pl.loop(1, columns)
        def _(shift):
            exchange(part, shift).wait()

    start_all(0)
    start_all(1)
    def remote(number, src, dst, device):
        return pltpu.make_async_remote_copy(
            src_ref=src,
            dst_ref=dst,
            send_sem=halo_send.at[number],
            recv_sem=halo_recv.at[number],
            device_id=device,
            device_id_type=MESH,
        )

    def row_copies(number, top, bottom, row):
        return [
            remote(
                number + place,
                top if up < 0 else bottom,
                row.at[place],
                (band_at(up), column_at(across)),
            )
            for place, (up, across) in enumerate(beside)
        ]

    def col_copies(number, to_left, to_right, col):
        return [
            remote(number + side, strip, col.at[side], (band, column_at(across)))
            for side, (strip, across) in enumerate(((to_left, -1), (to_right, 1)))
        ]

    has_above = jnp.where(band > 0, 1.0, 0.0)
    has_below = jnp.where(band < bands - 1, 1.0, 0.0)
    tile_lane = lax.broadcasted_iota(jnp.int32, (TILE, width), 1)
    low_lane = tile_lane < width // 2
    low_row = lax.broadcasted_iota(jnp.int32, (TILE, width), 0) < HALO
    low_rows = lax.broadcasted_iota(jnp.int32, (FINE, TILE, width), 1) < HALO
    above_at, below_at = 0, TILE + rows
    near = [(n, n) for n in range(TILE - HALO, TILE)]
    near += [(below_at + m, TILE + m) for m in range(HALO)]
    fine_near = sorted({n % FINE for n, _ in near})
    last = width - TILE
    side_rows = pl.ds(width, TILE)

    def turn(nat, field, fine):
        for f in fine:
            field[f, pl.ds(0, width), :] = nat[pl.ds(f, width, stride=FINE), :].T

    def ends_of(field):
        return field[:, pl.ds(0, TILE), :], field[:, pl.ds(last, TILE), :]

    many = (FINE + 1) // 2

    def paired(end):
        return jnp.concatenate([pltpu.roll(end[many:], HALO, 1), end[many - 1 : many]], axis=0)

    def strips_of(field):
        start, end = ends_of(field)
        low = low_rows[:many]
        return (
            jnp.where(low, start[:many], paired(start)),
            jnp.where(low, paired(end), end[:many]),
        )

    def halo_of(right, left):
        rest_right = pltpu.roll(right[: FINE - many], HALO, 1)
        rest_left = pltpu.roll(left[: FINE - many], HALO, 1)
        return jnp.concatenate(
            [
                jnp.where(low_rows[:many], right, left),
                jnp.where(low_rows[many:], rest_right, rest_left),
            ],
            axis=0,
        )

    def fill(nat, field, arrived_row, halo_columns, outside):
        for at, place, inside in ((above_at, 3, has_above), (below_at, 0, has_below)):
            right, middle, left = (arrived_row(place + k) for k in range(3))
            absent = (1.0 - inside) * outside
            nat[pl.ds(at, TILE), :] = middle * inside + absent
            side = jnp.where(low_lane, right, left) * inside + absent
            corner[pl.ds(TILE if at else 0, TILE), :] = side
        turn(nat, field, fine_near)
        turned = corner[...].T
        sides = jnp.where(low_row, turned[0:TILE, :], turned[last:width, :])
        field[:, side_rows, :] = halo_columns
        for n, lane in near:
            f, to = n % FINE, n // FINE
            moved = pltpu.roll(sides, (to - lane) % width, 1)
            field[f, side_rows, :] = jnp.where(tile_lane == to, moved, field[f, side_rows, :])

    pl.loop(0, 2)(lambda end: integrate(end * (chunks - 1)))
    corner[...] = jnp.zeros_like(corner)
    for number, nat in enumerate((nat_half, nat_source)):
        edge_first[0, number] = nat[pl.ds(TILE, TILE), :]
        edge_first[1, number] = nat[pl.ds(rows, TILE), :]
    first_rows = row_copies(0, edge_first.at[0], edge_first.at[1], row_first)
    for copy in first_rows:
        copy.start()
    pl.loop(1, chunks - 1)(integrate)
    turn(nat_half, raw, range(FINE))
    turn(nat_source, source, range(FINE))
    (raw_start, raw_end), (source_start, source_end) = ends_of(raw), ends_of(source)
    strip_first[0] = jnp.where(low_rows, raw_start, pltpu.roll(source_start, HALO, 1))
    strip_first[1] = jnp.where(low_rows, pltpu.roll(source_end, HALO, 1), raw_end)
    first_cols = col_copies(6, strip_first.at[0], strip_first.at[1], col_first)
    for copy in first_cols:
        copy.start()

    for block in range(blocks):
        value = map_v[me, first_row + block]
        owner_of[block] = jnp.where(value >= 0, value // slots, -1)
    for block in range(blocks):
        owner = owner_of[block]
        rank = jnp.int32(0)
        for before in range(block):
            rank = jnp.where(owner_of[before] == owner, 1, rank)
        t_clinic[block] = jnp.where(owner >= 0, owner * PAIR + rank, 0)

    @pl.loop(0, columns)
    def _(owner):
        first, second = jnp.int32(0), jnp.int32(0)
        for block in reversed(range(blocks)):
            mine = owner_of[block] == owner
            second = jnp.where(mine, first, second)
            first = jnp.where(mine, block, first)
        t_out[PAIR * owner] = first
        t_out[PAIR * owner + 1] = second

    @pl.loop(0, slots)
    def _(slot):
        place = jnp.int32(0)
        for entry in range(PAIR * columns):
            place = jnp.where(t_in[entry] == slot, entry, place)
        t_owner[slot] = place

    tiles = width // TILE + 1

    def tile_at(tile):
        return pl.ds(TILE * tile, TILE)

    def row_sum(value):
        before = jnp.concatenate([pltpu.roll(value[FINE - 1 :], 1, 2), value[: FINE - 1]], axis=0)
        after = jnp.concatenate([value[1:], pltpu.roll(value[:1], width - 1, 2)], axis=0)
        return before + after

    def put(field, tile, value):
        field[:, tile_at(tile + 1), :] = value
        if tile == tiles - 1:
            field[:, tile_at(0), :] = value
        if tile == 0:
            field[:, tile_at(tiles + 1), :] = value

    def col_sum(field, tile):
        start = TILE * (tile + 1)
        return field[:, pl.ds(start - 1, TILE), :] + field[:, pl.ds(start + 1, TILE), :]

    def sweeps(eta):
        for tile in range(tiles):
            here = tile_at(tile)
            rhs[:, here, :] = (SURFACE + 2.0 * half[:, here, :]) * eta[:, here, :] + source[
                :, here, :
            ]

        @pl.loop(0, ITERS)
        def _(iteration):
            for tile in range(tiles):
                here = tile_at(tile)
                value, weight = eta[:, here, :], half[:, here, :]
                scaled = value * weight
                around, scaled_around = row_sum(value), row_sum(scaled)
                put(g_eta, tile, value + 0.5 * around)
                put(g_half, tile, scaled + 0.5 * scaled_around)
                rest[:, here, :] = rhs[:, here, :] + weight * around + scaled_around
            for tile in range(tiles):
                here = tile_at(tile)
                total = rest[:, here, :] + col_sum(g_half, tile)
                total = total + half[:, here, :] * col_sum(g_eta, tile)
                eta[:, here, :] = total * inverse[:, here, :]

        for f in range(FINE):
            nat_half[pl.ds(f, width, stride=FINE), :] = eta[f, pl.ds(0, width), :].T

    def unpack(part, received, at, count):
        wait_all(part)
        for block in range(blocks):
            wet = jnp.where(map_v[me, first_row + block] >= 0, 1.0, 0.0)
            there = pl.ds(TILE + block * block_rows + at, count)
            nat_eta[there, :] = received[t_clinic[block]] * wet

    def send_back(part, end):
        sent, received = parts[part]

        @pl.loop(1, columns)
        def _(shift):
            peer = column_at(shift)
            for rank in range(PAIR):
                sent[PAIR * shift + rank] = end[t_out[PAIR * peer + rank]]
            exchange(part, shift).start()

        for rank in range(PAIR):
            received[PAIR * me + rank] = end[t_out[PAIR * me + rank]]

    unpack(0, recv_in_a, 0, IN_ROWS)
    turn(nat_eta, eta_a, range(FINE))
    strip_eta[0, 0], strip_eta[0, 1] = strips_of(eta_a)
    cols_a = col_copies(8, strip_eta.at[0, 0], strip_eta.at[0, 1], col_eta.at[0])
    for copy in cols_a:
        copy.start()


    unpack(1, recv_in_b, IN_ROWS, block_rows - IN_ROWS)
    rows_b = row_copies(10, nat_eta.at[pl.ds(TILE, TILE)], nat_eta.at[pl.ds(rows, TILE)], row_eta)
    for copy in rows_b:
        copy.start()
    turn(nat_eta, eta_b, range(FINE))
    strip_eta[1, 0], strip_eta[1, 1] = strips_of(eta_b)
    cols_b = col_copies(16, strip_eta.at[1, 0], strip_eta.at[1, 1], col_eta.at[1])
    for copy in cols_b:
        copy.start()

    for copy in first_rows + first_cols:
        copy.wait()
    raw_halo = jnp.where(low_rows, col_first[0], col_first[1])
    source_halo = pltpu.roll(jnp.where(low_rows, col_first[1], col_first[0]), HALO, 1)
    fill(nat_half, raw, lambda p: row_first[p, 0], raw_halo, -1.0)
    fill(nat_source, source, lambda p: row_first[p, 1], source_halo, 0.0)
    for tile in range(tiles):
        value = jnp.maximum(raw[:, tile_at(tile), :], 0.0)
        half[:, tile_at(tile), :] = value
        around = row_sum(value)
        put(g_half, tile, value + 0.5 * around)
        rest[:, tile_at(tile), :] = (SURFACE + 8.0 * value) + around
    for tile in range(tiles):
        diagonal = rest[:, tile_at(tile), :] + col_sum(g_half, tile)
        wet = raw[:, tile_at(tile), :] >= 0.0
        inverse[:, tile_at(tile), :] = jnp.where(wet, 1.0 / diagonal, 0.0)

    for copy in cols_a:
        copy.wait()
    eta_a[:, side_rows, :] = halo_of(col_eta[0, 0], col_eta[0, 1])
    sweeps(eta_a)
    for block in range(blocks):
        end_a[block] = nat_half[pl.ds(TILE + block * block_rows + OUT_ROW, OUT_ROWS), :]
    send_back(2, end_a)

    for copy in rows_b + cols_b:
        copy.wait()
    halo_b = halo_of(col_eta[1, 0], col_eta[1, 1])
    fill(nat_eta, eta_b, lambda p: row_eta[p], halo_b, 0.0)
    sweeps(eta_b)
    behind = block_rows - OUT_ROW - OUT_ROWS
    for block in range(blocks):
        start = TILE + block * block_rows
        end_b[block, pl.ds(0, behind), :] = nat_half[
            pl.ds(start + OUT_ROW + OUT_ROWS, behind), :
        ]
        end_b[block, pl.ds(behind, OUT_ROW), :] = nat_half[pl.ds(start, OUT_ROW), :]
    send_back(3, end_b)

    wait_all(2)

    @pl.loop(0, slots)
    def _(slot):
        eta_next[0, slot, pl.ds(OUT_ROW, OUT_ROWS), :] = recv_out_a[t_owner[slot]]

    wait_all(3)

    for slot in range(slots):
        value = recv_out_b[t_owner[slot]]
        eta_next[0, slot, pl.ds(OUT_ROW + OUT_ROWS, behind), :] = value[:behind]
        eta_next[0, slot, pl.ds(0, OUT_ROW), :] = value[behind:]


def solution(mesh):
    columns, bands = mesh.shape["bcol"], mesh.shape["brow"]

    def body(forcing, bottom_level, thickness, eta_prev, tropic_map):
        levels, rows, width = forcing.shape
        slots, block_rows = eta_prev.shape[1], eta_prev.shape[2]
        blocks = rows // block_rows
        sizes = (columns, bands, block_rows, rows, levels, slots, width)
        f32, dma = jnp.float32, pltpu.SemaphoreType.DMA

        def vmem(*shape):
            return pltpu.VMEM(shape, f32)

        def smem(*shape):
            return pltpu.SMEM(shape, jnp.int32)

        tall = width + TILE
        scratch = [
            pltpu.VMEM(forcing.shape, forcing.dtype),
            pltpu.VMEM((rows, width), jnp.int32),
            vmem(slots, block_rows, width),
        ]
        for count in (IN_ROWS, block_rows - IN_ROWS, OUT_ROWS, block_rows - OUT_ROWS):
            scratch += [vmem(PAIR * columns, count, width)] * 2
        scratch += [vmem(blocks, OUT_ROWS, width), vmem(blocks, block_rows - OUT_ROWS, width)]
        scratch += [vmem(FINE * width, width)] * 3 + [vmem(width, width)]
        scratch += [vmem(FINE, tall, width)] * 8
        scratch += [vmem(FINE, tall + 2 * TILE, width)] * 2
        scratch += [vmem(2, FINE, TILE, width)] * 2 + [vmem(2, 2, (FINE + 1) // 2, TILE, width)] * 2
        scratch += [vmem(2, 2, TILE, width), vmem(6, 2, TILE, width), vmem(6, TILE, width)]
        scratch += [smem(*tropic_map.shape[::-1]), pltpu.SMEM((levels,), f32)]
        scratch += [
            smem(PAIR * columns), smem(blocks), smem(PAIR * columns), smem(slots), smem(blocks)
        ]
        scratch += [dma((rows // CHUNK,))] + [dma] * 4 + [dma((4, columns))] * 2 + [dma((18,))] * 2
        return pl.pallas_call(
            functools.partial(kernel, sizes),
            out_shape=pltpu.VMEM(eta_prev.shape, f32),
            in_specs=[pl.BlockSpec(memory_space=pl.ANY)] * 5,
            out_specs=pl.BlockSpec(memory_space=pltpu.VMEM),
            scratch_shapes=scratch,
            compiler_params=pltpu.CompilerParams(
                collective_id=0, has_side_effects=True, vmem_limit_bytes=56 * 1024 * 1024
            ),
            cost_estimate=pl.CostEstimate(
                flops=60_000_000, bytes_accessed=18_000_000, transcendentals=0
            ),
        )(tropic_map.T, thickness, forcing, bottom_level, eta_prev)

    in_specs = (P(None, "brow", "bcol"), P("brow", "bcol"), P(), P("brow", "bcol", None, None), P())
    out_specs = P("brow", "bcol", None, None)
    return jax.shard_map(body, mesh=mesh, in_specs=in_specs, out_specs=out_specs, check_vma=False)
```
